128 devices in a mesh: dp: 32 (over x_lo, z, y), tensor: 4 (over x_hi, core).
Axes of the slice: x: 4 (x_hi: 2, x_lo: 2; x = x_hi * 2 + x_lo), y: 4, z: 4, core: 2. Of those that a mesh axis runs over, the one named last changes fastest.
Arguments:
- x_in: bfloat16 [32, 1024, 768], P('dp', 'tensor'), may hold values from -6 to 6
- segments: int32 [32, 1024], P('dp'), may hold values from 0 to 7, never falling along the last dimension, each value on 1 to 800 neighbouring positions
- attn_w: float32 [2, 4, 768, 768], P(None, None, 'dp', 'tensor'), may hold values from -0.21875 to 0.21875
- mlp_w: float32 [2, 2, 768, 4, 768], P(None, None, 'dp', None, 'tensor'), may hold values from -0.21875 to 0.21875
- in_bias: float32 [2, 7, 768], P(None, None, 'tensor'), may hold values from -3 to 3
- vectors: float32 [2, 6, 768], replicated, may hold values from 0.1 to 1.9
- mom_attn: float32 [2, 4, 768, 768], P(None, None, 'dp', 'tensor'), may hold values from -320 to 320
- mom_mlp: float32 [2, 2, 768, 4, 768], P(None, None, 'dp', None, 'tensor'), may hold values from -320 to 320
- mom_bias: float32 [2, 7, 768], P(None, None, 'tensor'), may hold values from -320 to 320
- mom_vec: float32 [2, 6, 768], replicated, may hold values from -512 to 512
- cotangent: float32 [32, 1024, 768], P('dp', 'tensor'), may hold values from -6 to 6
Outputs:
- out_act: float32 [32, 1024, 768], P('dp', 'tensor')
- grad_in: float32 [32, 1024, 768], P('dp', 'tensor')
- new_mom_attn: float32 [2, 4, 768, 768], P(None, None, 'dp', 'tensor')
- new_attn_w: float32 [2, 4, 768, 768], P(None, None, 'dp', 'tensor')
- new_mom_mlp: float32 [2, 2, 768, 4, 768], P(None, None, 'dp', None, 'tensor')
- new_mlp_w: float32 [2, 2, 768, 4, 768], P(None, None, 'dp', None, 'tensor')
- new_mom_bias: float32 [2, 7, 768], P(None, None, 'tensor')
- new_in_bias: float32 [2, 7, 768], P(None, None, 'tensor')
- new_mom_vec: float32 [2, 6, 768], replicated
- new_vectors: float32 [2, 6, 768], replicated
The draws below stay inside these ranges and needn't reach their ends.
Inputs may be any that keep to these rules, and one draw needn't show every extreme that they name: `segments`: in every sequence segment numbers never fall, every document has 1 to 800 tokens, and one has exactly 800.
All inputs are finite; a program needn't handle non-finite values.
Results may differ from the reference program's by a relative error of at most 0.018.
The reference program's roundings to bfloat16 on the way count: a program that leaves them out, or rounds other values in their place, can miss the bound.
Values may be sent and summed in bfloat16 or wider, within the bound.
No kernel may reach another device: no remote copies, remote signals or barrier semaphores. Data moves between devices by JAX's collectives and lax.ppermute only.
A program may use at most 192 MiB of HBM per device.

```python
import math
import jax
import jax.numpy as jnp
import numpy as np
from jax import lax

D = 768
HEADS = 12
FF = 3072
HD = 64
ROT = 16
LAYERS = 2
NS_STEPS = 5
SEQ = 1024
NSEQ = 32
TOKENS = 32768
MOST = 800
DOCS = 8


def block_levels(rng, extent, shards, low, top_value):
    def one(dim, shards_of):
        heights = jax.random.uniform(jax.random.fold_in(jax.random.fold_in(rng, 6), dim), (shards_of,), jnp.float32, low / len(shards), top_value / len(shards))
        return jnp.repeat(jnp.exp(heights), extent[dim] // shards_of).reshape((-1,) + (1,) * (len(extent) - dim - 1))

    loudness = one(*shards[0])
    for cut in shards[1:]:
        loudness = loudness * one(*cut)
    return loudness


def split_up(amount, total, most, slope):
    portions = [(1 << 20) // math.isqrt(standing ** slope) + 1 for standing in range(2, amount + 1)]
    spare, holding = total - most - (amount - 1), [1] * (amount - 1)
    while spare > 0:
        candidates = [i for i in range(amount - 1) if holding[i] < most]
        mass, budget = sum([portions[i] for i in candidates]), spare
        for i in candidates:
            addition = min(most - holding[i], max(1, budget * portions[i] // mass), spare)
            holding[i] = holding[i] + addition
            spare = spare - addition
    return np.array([most] + holding)


def uneven(own_key, amount, total, limit, skew):
    if amount == 2:
        one = jax.random.randint(own_key, (), max(1, total - limit), min(limit, total - 1) + 1)
        return jnp.stack([one, total - one])
    sizes = jnp.asarray(split_up(amount, total, limit, skew), jnp.int32)
    pairs = (amount - 1) // 2
    giver, receiver = sizes[1:1 + 2 * pairs:2], sizes[2:2 + 2 * pairs:2]
    margin = jnp.minimum(giver - 1, limit - receiver)
    moved = jax.random.randint(jax.random.fold_in(own_key, 1), (pairs,), 0, 1 << 20) % (margin + 1)
    sizes = sizes.at[1:1 + 2 * pairs:2].set(giver - moved).at[2:2 + 2 * pairs:2].set(receiver + moved)
    return sizes[jax.random.permutation(jax.random.fold_in(own_key, 2), amount)]


def scatter_about(rng, extent, deviation, bound, cuts=(), kind=jnp.bfloat16):
    result = deviation * jax.random.normal(rng, extent, jnp.float32)
    if cuts:
        result = result * block_levels(rng, extent, cuts, -0.22, 0.18)
    return jnp.clip(result, -bound, bound).astype(kind)


def setup_inputs(seed: int = 0) -> dict:
    key_of = jax.random.split(jax.random.key(seed), 12)
    x_in = scatter_about(key_of[0], (NSEQ, SEQ, D), 1.0, 6.0, ((0, 32), (1, 4)))
    segments = jax.vmap(lambda own: jnp.searchsorted(jnp.cumsum(uneven(own, DOCS, SEQ, MOST, 0)), jnp.arange(SEQ), side="right"))(jax.random.split(key_of[1], NSEQ)).reshape((NSEQ, SEQ)).astype(jnp.int32)
    attn_w = scatter_about(key_of[2], (LAYERS, 4, D, D), D ** -0.5, 0.21875, ((2, 32), (3, 4)), jnp.float32)
    mlp_w = scatter_about(key_of[3], (LAYERS, 2, D, 4, D), D ** -0.5, 0.21875, ((2, 32), (4, 4)), jnp.float32)
    in_bias = scatter_about(key_of[4], (LAYERS, 7, D), 0.5, 3.0, ((2, 4),), jnp.float32)
    vectors = jnp.clip(1.0 + 0.18 * jax.random.normal(key_of[5], (LAYERS, 6, D), jnp.float32), 0.1, 1.9)
    mom_attn = scatter_about(key_of[6], (LAYERS, 4, D, D), (0.3 * TOKENS ** 0.5), 320.0, ((2, 32), (3, 4)), jnp.float32)
    mom_mlp = scatter_about(key_of[7], (LAYERS, 2, D, 4, D), (0.3 * TOKENS ** 0.5), 320.0, ((2, 32), (4, 4)), jnp.float32)
    mom_bias = scatter_about(key_of[8], (LAYERS, 7, D), (0.3 * TOKENS ** 0.5), 320.0, ((2, 4),), jnp.float32)
    mom_vec = scatter_about(key_of[9], (LAYERS, 6, D), (0.5 * TOKENS ** 0.5), 512.0, (), jnp.float32)
    cotangent = scatter_about(key_of[10], (NSEQ, SEQ, D), 1.0, 6.0, ((0, 32), (1, 4)), jnp.float32)
    return {"x_in": x_in, "segments": segments, "attn_w": attn_w, "mlp_w": mlp_w, "in_bias": in_bias, "vectors": vectors, "mom_attn": mom_attn, "mom_mlp": mom_mlp, "mom_bias": mom_bias, "mom_vec": mom_vec, "cotangent": cotangent}


@jax.custom_vjp
def low(v):
    return lax.optimization_barrier(v.astype(jnp.bfloat16)).astype(jnp.float32)

@jax.custom_vjp
def low_back(v):
    return v

def low_keep(v):
    return (low(v), None)

def low_pass(kept, grad):
    return (grad,)

def back_keep(v):
    return (v, None)

def back_low(kept, grad):
    return (low(grad),)
low.defvjp(low_keep, low_pass)
low_back.defvjp(back_keep, back_low)
EPS_NORM = 1e-05
EPS_ORTH = 1e-07
COEF_A = 3.4445
COEF_B = -4.775
COEF_C = 2.0315
MOMENTUM = 0.95
STEP_SCALE = 0.4
RATE_VEC = 0.5
NEG_FILL = -1e+30
PRECISE = lax.Precision.HIGHEST

def normalize(stream, gain_row, shift_row):
    center = stream - lax.optimization_barrier(jnp.mean(stream, -1, keepdims=True))
    inverse = lax.rsqrt(lax.optimization_barrier(jnp.mean(center * center, -1, keepdims=True)) + EPS_NORM)
    return center * inverse * gain_row + shift_row

def rope_tables(segments):
    length = segments.shape[-1]
    earlier = lax.optimization_barrier(jnp.sum((segments[:, None, :] < segments[:, :, None]).astype(jnp.int32), -1))
    places = jnp.arange(length, dtype=jnp.int32)[None, :] - earlier
    frequency = 10000.0 ** (jnp.arange(ROT // 2, dtype=jnp.float32) * (-2.0 / ROT))
    angles = places.astype(jnp.float32)[:, :, None] * frequency
    return (jnp.cos(angles)[:, :, None, :], jnp.sin(angles)[:, :, None, :])

def rotate(heads_in, cosine_table, sine_table):
    half_rot = ROT // 2
    leading = heads_in[..., :half_rot]
    trailing = heads_in[..., half_rot:ROT]
    return jnp.concatenate([leading * cosine_table - trailing * sine_table, trailing * cosine_table + leading * sine_table, heads_in[..., ROT:]], -1)

def attend(packed):
    queries, key_rows, values, labels = packed
    length = queries.shape[0]
    places = jnp.arange(length, dtype=jnp.int32)
    allowed = (labels[:, None] == labels[None, :]) & (places[:, None] >= places[None, :])
    scores = low_back(jnp.einsum('qhd,khd->hqk', queries, key_rows, precision=PRECISE) * queries.shape[-1] ** (-0.5))
    scores = jnp.where(allowed[None], scores, NEG_FILL)
    shifted = jnp.exp(scores - lax.optimization_barrier(jnp.max(scores, -1, keepdims=True)))
    probability = shifted / lax.optimization_barrier(jnp.sum(shifted, -1, keepdims=True))
    return jnp.einsum('hqk,khd->qhd', low(probability), values, precision=PRECISE)

def orthogonalize(matrix):
    gram_matrix = jnp.dot(matrix, matrix.T, precision=PRECISE)
    frob_norm = jnp.sqrt(jnp.trace(gram_matrix)) + EPS_ORTH
    current = matrix / frob_norm
    gram_matrix = gram_matrix / (frob_norm * frob_norm)
    for ns_step in range(NS_STEPS):
        if ns_step > 0:
            gram_matrix = jnp.dot(current, current.T, precision=PRECISE)
        polynomial = COEF_B * gram_matrix + COEF_C * jnp.dot(gram_matrix, gram_matrix, precision=PRECISE)
        current = COEF_A * current + jnp.dot(polynomial, current, precision=PRECISE)
    return current

def reference(x_in, segments, attn_w, mlp_w, in_bias, vectors, mom_attn, mom_mlp, mom_bias, mom_vec, cotangent):
    cosine_table, sine_table = rope_tables(segments)

    def forward(stream, attn_all, mlp_all, bias_all, vector_all):
        seq_count, length, model_width = stream.shape
        for layer_index in range(LAYERS):
            attn_low = low(attn_all[layer_index])
            mlp_low = low(mlp_all[layer_index])
            bias_rows = bias_all[layer_index]
            vector_rows = vector_all[layer_index]
            first_normed = low(normalize(stream, vector_rows[0], vector_rows[1]))
            second_normed = low(normalize(stream, vector_rows[2], vector_rows[3]))
            projected = low_back(jnp.einsum('nsd,mdh->nsmh', first_normed, attn_low[:3], precision=PRECISE) + bias_rows[:3])
            head_view = projected.reshape(seq_count, length, 3, HEADS, HD)
            queries = low(rotate(head_view[:, :, 0], cosine_table, sine_table))
            key_rows = low(rotate(head_view[:, :, 1], cosine_table, sine_table))
            values = low(head_view[:, :, 2])
            mixed_heads = lax.map(jax.checkpoint(attend), (queries, key_rows, values, segments))
            mixed_heads = low(low_back(mixed_heads.reshape(seq_count, length, model_width)))
            pre_act = low_back(jnp.einsum('nsd,drc->nsrc', second_normed, mlp_low[0], precision=PRECISE) + bias_rows[3:])
            hidden = low(jax.nn.gelu(pre_act, approximate=False))
            branch = low_back(jnp.einsum('nsh,dh->nsd', mixed_heads, attn_low[3], precision=PRECISE) + jnp.einsum('nsrc,drc->nsd', hidden, mlp_low[1], precision=PRECISE))
            stream = stream + branch + vector_rows[4] + vector_rows[5]
        return stream
    out_act, pullback = jax.vjp(forward, x_in.astype(jnp.float32), attn_w, mlp_w, in_bias, vectors)
    grad_in, grad_attn, grad_mlp, grad_bias, grad_vec = pullback(cotangent)
    new_mom_attn = MOMENTUM * mom_attn + grad_attn
    new_mom_mlp = MOMENTUM * mom_mlp + grad_mlp
    new_mom_bias = MOMENTUM * mom_bias + grad_bias
    new_mom_vec = MOMENTUM * mom_vec + grad_vec
    attn_orth = jnp.stack([jnp.stack([orthogonalize(new_mom_attn[layer_index, matrix_index]) for matrix_index in range(4)]) for layer_index in range(LAYERS)])
    mlp_orth = jnp.stack([jnp.stack([orthogonalize(new_mom_mlp[layer_index, matrix_index].reshape(D, FF)).reshape(D, 4, D) for matrix_index in range(2)]) for layer_index in range(LAYERS)])
    new_attn_w = attn_w - STEP_SCALE * math.sqrt(D) * attn_orth
    new_mlp_w = mlp_w - STEP_SCALE * math.sqrt(FF) * mlp_orth
    tokens_all = x_in.shape[0] * x_in.shape[1]
    vec_rate = RATE_VEC / math.sqrt(tokens_all)
    new_in_bias = in_bias - vec_rate * new_mom_bias
    new_vectors = vectors - vec_rate * new_mom_vec
    return (out_act, grad_in, new_mom_attn, new_attn_w, new_mom_mlp, new_mlp_w, new_mom_bias, new_in_bias, new_mom_vec, new_vectors)
```

```python
import math

import jax
import jax.numpy as jnp
from jax import lax
from jax.sharding import PartitionSpec as P

D = 768
FF = 3072
HD = 64
ROT = 16
NS_STEPS = 5
HEADS_HERE = 3
COLS = 192
CHUNK = 24
WIDE = 2304

EPS_NORM = 1e-05
EPS_ORTH = 1e-07
COEF_A = 3.4445
COEF_B = -4.775
COEF_C = 2.0315
MOMENTUM = 0.95
STEP_SCALE = 0.4
RATE_VEC = 0.5
NEG_FILL = -1e30

BF = jnp.bfloat16
F32 = jnp.float32


def dp_swap(value, mask):
    return lax.ppermute(value, "dp", [(i, i ^ mask) for i in range(32)])


def tensor_swap(value, mask):
    return lax.ppermute(value, "tensor", [(i, i ^ mask) for i in range(4)])


def dp_place():
    me = lax.axis_index("dp")
    return me // 16, (me // 4) % 4, me % 4


def swap_four(pieces, unit):
    return [pieces[0]] + [dp_swap(pieces[s], s * unit) for s in (1, 2, 3)]


def gather_rows(shard):
    spread = jnp.broadcast_to(shard[None], (32,) + shard.shape)
    return lax.all_to_all(spread, "dp", 0, 0, tiled=True).reshape(D, shard.shape[1])


def scatter_rows(full):
    arrived = lax.all_to_all(full.reshape(32, CHUNK, full.shape[1]), "dp", 0, 0, tiled=True)
    return jnp.sum(arrived.astype(F32), 0)


def gather_tokens(mine):
    far = tensor_swap(mine, 2)
    near = tensor_swap(mine, 1)
    diagonal = tensor_swap(far, 1)
    return jnp.stack([mine, near, far, diagonal])


def scatter_tokens(partial):
    arrived = tensor_swap(partial[1::2].astype(BF), 1)
    pair = partial[0::2] + arrived.astype(F32)
    return pair[0] + tensor_swap(pair[1].astype(BF), 2).astype(F32)


def standardize(stream):
    center = stream - jnp.mean(stream, -1, keepdims=True)
    inverse = lax.rsqrt(jnp.mean(center * center, -1, keepdims=True) + EPS_NORM)
    return center * inverse, inverse


def rope_tables(labels, places):
    kinds = jnp.arange(8, dtype=jnp.int32)
    below = jnp.sum((labels[None, :] < kinds[:, None]).astype(jnp.int32), 1)
    earlier = jnp.sum(jnp.where(labels[None, :] == kinds[:, None], below[:, None], 0), 0)
    frequency = 10000.0 ** (jnp.arange(ROT // 2, dtype=F32) * (-2.0 / ROT))
    angles = (places - earlier).astype(F32)[None, :] * frequency[:, None]
    return jnp.cos(angles).T[:, None, :], jnp.sin(angles).T[:, None, :]


def rotate(heads_in, cosine, sine):
    half = ROT // 2
    leading, trailing = heads_in[..., :half], heads_in[..., half:ROT]
    return jnp.concatenate(
        [leading * cosine - trailing * sine, trailing * cosine + leading * sine, heads_in[..., ROT:]],
        -1,
    )


def gelu_and_slope(pre_act):
    below = 0.5 * (1.0 + jax.scipy.special.erf(pre_act * 0.7071067811865476))
    return (
        (pre_act * below).astype(BF),
        below + pre_act * jnp.exp(-0.5 * pre_act * pre_act) * 0.3989422804014327,
    )


def mm(spec, left, right):
    return jnp.einsum(spec, left, right, preferred_element_type=F32)


def attend_forward(queries, keys, values, allowed):
    factor = HD ** (-0.5)
    outs, totals = [], []
    for start in range(0, 1024, 512):
        rows = slice(start, start + 512)
        scores = mm("qhd,khd->hqk", queries[rows], keys) * factor
        scores = jnp.where(allowed[None, rows], scores, NEG_FILL)
        row_max = jnp.max(scores, -1, keepdims=True)
        shifted = jnp.exp(scores - row_max)
        row_total = jnp.sum(shifted, -1, keepdims=True)
        probability = (shifted / row_total).astype(BF)
        outs.append(mm("hqk,khd->qhd", probability, values))
        totals.append(row_max + jnp.log(row_total))
    return jnp.concatenate(outs, 0), jnp.concatenate(totals, 1)


def attend_backward(queries, keys, values, allowed, log_total, d_mixed):
    factor = HD ** (-0.5)
    query_grads = []
    key_grad = value_grad = 0.0
    for start in range(0, 1024, 512):
        rows = slice(start, start + 512)
        scores = mm("qhd,khd->hqk", queries[rows], keys) * factor
        probability = jnp.where(allowed[None, rows], jnp.exp(scores - log_total[:, rows]), 0.0)
        prob_grad = mm("qhd,khd->hqk", d_mixed[rows], values)
        score_grad = (
            probability * (prob_grad - jnp.sum(probability * prob_grad, -1, keepdims=True))
        ).astype(BF)
        query_grads.append(mm("hqk,khd->qhd", score_grad, keys) * factor)
        key_grad = key_grad + mm("hqk,qhd->khd", score_grad, queries[rows]) * factor
        value_grad = value_grad + mm("hqk,qhd->khd", probability.astype(BF), d_mixed[rows])
    return jnp.concatenate(query_grads, 0), key_grad, value_grad


def forward_layer(stream, weights, bias_rows, vector_rows, cosine, sine, allowed):
    scaled, inverse = standardize(stream)
    scaled_all = gather_tokens(scaled.astype(jnp.float16)).reshape(1024, D).astype(F32)
    first = (scaled_all * vector_rows[0] + vector_rows[1]).astype(BF)
    second = (scaled_all * vector_rows[2] + vector_rows[3]).astype(BF)
    projected = mm("sd,dh->sh", first, weights[0]) + bias_rows[:3].reshape(-1)
    view = projected.reshape(1024, 3, HEADS_HERE, HD)
    queries = rotate(view[:, 0], cosine, sine).astype(BF)
    keys = rotate(view[:, 1], cosine, sine).astype(BF)
    values = view[:, 2].astype(BF)
    mixed, log_total = attend_forward(queries, keys, values, allowed)
    mixed = mixed.reshape(1024, COLS).astype(BF)
    pre_act = mm("sd,dh->sh", second, weights[1]) + bias_rows[3:].reshape(-1)
    hidden, slope = gelu_and_slope(pre_act)
    inner = jnp.concatenate([hidden, mixed], 1)
    branch = scatter_tokens(mm("sh,dh->sd", inner, weights[2]).reshape(4, 256, D))
    record = (scaled, inverse, scaled_all, first, second, queries, keys, values, log_total, slope, inner)
    return record, stream + branch + vector_rows[4] + vector_rows[5]


def backward_layer(upstream, outer, record, weights, vector_rows, cosine, sine, allowed):
    scaled, inverse, scaled_all, first, second, queries, keys, values, log_total, slope, inner = record
    d_inner = mm("sd,dh->sh", outer, weights[2])
    d_mixed = d_inner[:, 768:].astype(BF)
    d_pre = (d_inner[:, :768] * slope).astype(BF)
    grad_rest = jnp.concatenate(
        [mm("sd,sh->dh", outer, inner).astype(BF), mm("sd,sh->dh", second, d_pre).astype(BF)], 1
    )
    rest = scatter_rows(grad_rest)
    query_grad, key_grad, value_grad = attend_backward(
        queries, keys, values, allowed, log_total, d_mixed.reshape(1024, HEADS_HERE, HD)
    )
    d_proj = jnp.stack(
        [rotate(query_grad, cosine, -sine), rotate(key_grad, cosine, -sine), value_grad], 1
    ).astype(BF).reshape(1024, 576)
    grad_proj = mm("sd,sh->dh", first, d_proj).astype(BF)
    d_first = mm("sh,dh->sd", d_proj, weights[0])
    d_second = mm("sh,dh->sd", d_pre, weights[1])
    weighted = scatter_tokens(
        (d_first * vector_rows[0] + d_second * vector_rows[2]).reshape(4, 256, D)
    )
    new_upstream = upstream + inverse * (
        weighted
        - jnp.mean(weighted, -1, keepdims=True)
        - scaled * jnp.mean(weighted * scaled, -1, keepdims=True)
    )
    wide = scaled_all
    small = jnp.concatenate(
        [
            jnp.sum(d_first * wide, 0),
            jnp.sum(d_first, 0),
            jnp.sum(d_second * wide, 0),
            jnp.sum(d_second, 0),
            jnp.sum(upstream, 0),
            jnp.sum(d_proj.astype(F32), 0),
            jnp.sum(d_pre.astype(F32), 0),
            jnp.zeros((192,), F32),
        ]
    ).reshape(7, D)
    near, rest = lax.optimization_barrier(
        (jnp.concatenate([grad_proj, two_terms(small.T)], 1), rest)
    )
    near = scatter_rows(near)
    grads = jnp.concatenate([rest[:, :960], near[:, :576], rest[:, 960:]], 1)
    return new_upstream, grads, near[:, 576:583] + near[:, 583:]


def two_terms(value):
    upper = value.astype(BF)
    return jnp.concatenate([upper, (value - upper.astype(F32)).astype(BF)], 1)


def pack_shard(attn, mlp):
    up = mlp[0].reshape(CHUNK, 768)
    down = mlp[1].reshape(CHUNK, 768)
    return jnp.concatenate([down, attn[3], attn[0], attn[1], attn[2], up], 1)


def unpack_shard(wide):
    attn = jnp.stack([wide[:, 960:1152], wide[:, 1152:1344], wide[:, 1344:1536], wide[:, 768:960]])
    mlp = jnp.stack([wide[:, 1536:], wide[:, :768]]).reshape(2, CHUNK, 4, COLS)
    return attn, mlp


def high(left, right):
    return jnp.dot(left, right, precision=lax.Precision.HIGH)


def orthogonal_blocks(moms, small):
    x, z, y = dp_place()
    sends = []
    for to_x in range(2):
        for to_z in range(4):
            wide = moms[to_z // 2]
            if to_x == 0:
                sends.append(wide[:, 1536:] if to_z % 2 == 0 else wide[:, :768])
            else:
                pair = wide[:, 960:1344] if to_z % 2 == 0 else jnp.concatenate([wide[:, 1344:1536], wide[:, 768:960]], 1)
                sends.append(jnp.pad(pair, ((0, 0), (0, 384))))
    sends = jnp.stack(sends).astype(BF)
    groups = [[i + y_place for i in range(0, 32, 4)] for y_place in range(4)]
    rows = lax.all_to_all(sends, "dp", 0, 0, tiled=True, axis_index_groups=groups)
    rows = rows.reshape(192, 768)
    far = tensor_swap(rows, 2)
    whole = jnp.stack(swap_four([jnp.stack([rows, far])] * 4, 1))
    half = y // 2
    column = jnp.arange(768) // COLS
    whole = jnp.where((x == 0) | (column == half), whole, jnp.zeros((), BF))
    mine = whole[:, 0].reshape(768, 768)
    other = whole[:, 1].reshape(768, 768)
    gram = mm("ac,bc->ab", mine, mine) + mm("ac,bc->ab", other, other)
    gram = gram + tensor_swap(gram, 1)
    scale = 1.0 / (jnp.sqrt(jnp.trace(gram)) + EPS_ORTH)
    which = jnp.where(x == 0, y, half)
    block = jnp.zeros((768, COLS), BF)
    for i in range(4):
        block = jnp.where(which == i, mine[:, i * COLS : (i + 1) * COLS], block)
    current = block.astype(F32) * scale
    gram = gram * (scale * scale)
    for ns_step in range(NS_STEPS):
        mixer = COEF_B * gram + COEF_C * high(gram, gram)
        current = COEF_A * current + high(mixer, current)
        if ns_step < NS_STEPS - 1:
            gram = COEF_A * gram + high(mixer, gram)
            gram = COEF_A * gram + high(gram, mixer)
    result = current.astype(BF).reshape(4, 8, CHUNK, COLS)
    result = jnp.stack([lax.dynamic_index_in_dim(result, y ^ s, 0, keepdims=False) for s in range(4)], 1)
    spread = jnp.broadcast_to(two_terms(small)[None], (32, CHUNK, 28))
    result = jnp.concatenate([result.reshape(32, CHUNK, COLS), spread], 2)
    back = lax.all_to_all(result, "dp", 0, 0, tiled=True).astype(F32)
    small = (back[:, :, 192:206] + back[:, :, 206:]).reshape(D, 14)
    back = back[:, :, :192].reshape(2, 4, 4, CHUNK, COLS)
    wides = []
    for layer in range(2):
        up = [back[0, 2 * layer, i] for i in range(4)]
        down = [back[0, 2 * layer + 1, i] for i in range(4)]
        query, key = back[1, 2 * layer, 0], back[1, 2 * layer, 2]
        value, output = back[1, 2 * layer + 1, 0], back[1, 2 * layer + 1, 2]
        wides.append(jnp.concatenate(down + [output, query, key, value] + up, 1))
    return wides, small


def per_device(
    x_in, segments, attn_w, mlp_w, in_bias, vectors, mom_attn, mom_mlp, mom_bias, mom_vec, cotangent
):
    me = lax.axis_index("tensor")
    order = [me ^ s for s in range(4)]
    places = jnp.concatenate([i * 256 + jnp.arange(256, dtype=jnp.int32) for i in order])
    labels = jnp.concatenate([lax.dynamic_slice(segments[0], (i * 256,), (256,)) for i in order])
    cosine, sine = rope_tables(labels, places)
    allowed = (labels[:, None] == labels[None, :]) & (places[:, None] >= places[None, :])
    shards = [pack_shard(attn_w[layer], mlp_w[layer]).astype(BF) for layer in range(2)]
    near = gather_rows(shards[0][:, 960:1536])
    rest, near = lax.optimization_barrier((jnp.concatenate([shards[0][:, 1536:], shards[0][:, :960]], 1), near))
    rest = gather_rows(rest)
    later, rest = lax.optimization_barrier((shards[1], rest))
    later = gather_rows(later)
    weights = [
        (near, rest[:, :768], rest[:, 768:]),
        (later[:, 960:1536], later[:, 1536:], later[:, :960]),
    ]
    stream = x_in[0].astype(F32)
    upstream = cotangent[0]
    saved = []
    for layer in range(2):
        if layer == 1:
            stream, weights[1] = lax.optimization_barrier((stream, weights[1]))
        record, stream = forward_layer(
            stream, weights[layer], in_bias[layer], vectors[layer], cosine, sine, allowed
        )
        saved.append(record)
    grads, smalls = [None, None], [None, None]
    for layer in (1, 0):
        outer = gather_tokens(upstream.astype(BF)).reshape(1024, D)
        upstream, grads[layer], smalls[layer] = backward_layer(
            upstream, outer, saved[layer], weights[layer], vectors[layer], cosine, sine, allowed
        )
    shared = jnp.concatenate([s[:, :5] for s in smalls], 1)
    for mask in (1, 2):
        shared = shared + tensor_swap(shared, mask)
    small = jnp.concatenate([shared] + [s[:, 5:] for s in smalls], 1)
    moms = [
        MOMENTUM * pack_shard(mom_attn[layer], mom_mlp[layer]) + grads[layer] for layer in range(2)
    ]
    orth, small = orthogonal_blocks(moms, small)
    vec_total = small[:, :10].T.reshape(2, 5, D)
    vec_total = jnp.concatenate([vec_total, vec_total[:, 4:]], 1)
    bias_total = small[:, 10:].T.reshape(2, 2 * D)[:, :1344].reshape(2, 7, COLS)
    new_mom_attn, new_mom_mlp, new_attn_w, new_mlp_w = [], [], [], []
    for layer in range(2):
        a, m = unpack_shard(moms[layer])
        new_mom_attn.append(a)
        new_mom_mlp.append(m)
        a, m = unpack_shard(orth[layer])
        new_attn_w.append(attn_w[layer] - STEP_SCALE * math.sqrt(D) * a)
        new_mlp_w.append(mlp_w[layer] - STEP_SCALE * math.sqrt(FF) * m)
    new_mom_bias = MOMENTUM * mom_bias + bias_total
    new_mom_vec = MOMENTUM * mom_vec + vec_total
    vec_rate = RATE_VEC / math.sqrt(32768)
    return (
        stream[None],
        upstream[None],
        jnp.stack(new_mom_attn),
        jnp.stack(new_attn_w),
        jnp.stack(new_mom_mlp),
        jnp.stack(new_mlp_w),
        new_mom_bias,
        in_bias - vec_rate * new_mom_bias,
        new_mom_vec,
        vectors - vec_rate * new_mom_vec,
    )


def solution(mesh):
    placed = (
        P("dp", "tensor", None),
        P("dp", None),
        P(None, None, "dp", "tensor"),
        P(None, None, "dp", None, "tensor"),
        P(None, None, "tensor"),
        P(),
        P(None, None, "dp", "tensor"),
        P(None, None, "dp", None, "tensor"),
        P(None, None, "tensor"),
        P(),
        P("dp", "tensor", None),
    )
    return jax.shard_map(
        per_device,
        mesh=mesh,
        in_specs=placed,
        out_specs=(
            P("dp", "tensor", None),
            P("dp", "tensor", None),
            P(None, None, "dp", "tensor"),
            P(None, None, "dp", "tensor"),
            P(None, None, "dp", None, "tensor"),
            P(None, None, "dp", None, "tensor"),
            P(None, None, "tensor"),
            P(None, None, "tensor"),
            P(),
            P(),
        ),
        check_vma=False,
    )
```

```python
import functools
import math

import jax
import jax.numpy as jnp
import numpy as np
from jax import lax
from jax.experimental import pallas as pl
from jax.experimental.pallas import tpu as pltpu
from jax.sharding import PartitionSpec as P

D = 768
FF = 3072
HD = 64
ROT = 16
CHUNK = 24
EPS_NORM = 1e-05
MOMENTUM = 0.95
STEP_SCALE = 0.4
RATE_VEC = 0.5
COLS = 192
HEADS_HERE = 3
NS_STEPS = 5
EPS_ORTH = 1e-07
COEF_A = 3.4445
COEF_B = -4.775
COEF_C = 2.0315
NEG_FILL = -1e30
BF = jnp.bfloat16
F32 = jnp.float32
VMEM = pltpu.VMEM


def dot_nn(a, b):
    return lax.dot_general(a, b, (((1,), (0,)), ((), ())), preferred_element_type=F32)


def dot_nt(a, b):
    return lax.dot_general(a, b, (((1,), (1,)), ((), ())), preferred_element_type=F32)


def dot_tn(a, b):
    return lax.dot_general(a, b, (((0,), (0,)), ((), ())), preferred_element_type=F32)


def call(kernel, outs, ins, scratch=(), grid=None, in_specs=None, out_specs=None, flops=0, limit=60):
    whole = pl.BlockSpec(memory_space=VMEM)
    kwargs = {} if grid is None else dict(grid=grid)
    return pl.pallas_call(
        kernel,
        out_shape=[jax.ShapeDtypeStruct(s, d) for s, d in outs],
        in_specs=in_specs or [whole] * len(ins),
        out_specs=out_specs or [whole] * len(outs),
        scratch_shapes=list(scratch),
        compiler_params=pltpu.CompilerParams(vmem_limit_bytes=limit * 1024 * 1024),
        cost_estimate=pl.CostEstimate(flops=flops, bytes_accessed=1 << 16, transcendentals=0),
        **kwargs,
    )(*ins)


SMEM_SPEC = pl.BlockSpec(memory_space=pltpu.SMEM)
NEAR_SPEC = pl.BlockSpec((D, D), lambda *_: (0, 2))
WIDE = 2304


def head_mask(h):
    lane = lax.broadcasted_iota(jnp.int32, (1, COLS), 1)
    return ((lane >= h * HD) & (lane < (h + 1) * HD)).astype(BF)


def allowed_t(start_row, i, width):
    key = lax.broadcasted_iota(jnp.int32, (width, 256), 0)
    query = lax.broadcasted_iota(jnp.int32, (width, 256), 1) + i * 256
    return (key >= start_row) & (key <= query)


def rope_at(cos_ref, sin_ref, there):
    lane = lax.broadcasted_iota(jnp.int32, (8, COLS), 1) % HD
    angle = lax.broadcasted_iota(jnp.int32, (8, COLS), 0)
    spread = ((lane < ROT) & (lane % (ROT // 2) == angle)).astype(F32)
    rest = (lax.broadcasted_iota(jnp.int32, (1, COLS), 1) % HD >= ROT).astype(F32)
    exact = dict(preferred_element_type=F32, precision=lax.Precision.HIGHEST)
    over = (((0,), (0,)), ((), ()))
    cosine = lax.dot_general(cos_ref[:, there], spread, over, **exact) + rest
    return cosine, lax.dot_general(sin_ref[:, there], spread, over, **exact)


def attend_forward_kernel(
    me_ref, first0_ref, first1_ref, first2_ref, first3_ref, w_ref, bias_ref, turn_ref, cos_ref, sin_ref, start_ref,
    q_ref, k_ref, v_ref, lse_ref, mixed_ref,
):
    me = me_ref[0]
    turn = turn_ref[...]
    wq, wk, wv = w_ref[:, COLS : 2 * COLS], w_ref[:, 2 * COLS : 3 * COLS], w_ref[:, 3 * COLS :]
    wqt = dot_nn(wq, turn).astype(BF)
    wkt = dot_nn(wk, turn).astype(BF)
    bias = bias_ref[:3]
    turned = lax.dot_general(
        bias[:2], turn.astype(F32), (((1,), (0,)), ((), ())),
        preferred_element_type=F32, precision=lax.Precision.HIGHEST,
    )
    for a in range(4):
        there = pl.ds(pl.multiple_of((me ^ a) * 256, 256), 256)
        x = (first0_ref, first1_ref, first2_ref, first3_ref)[a][...]
        cosine, sine = rope_at(cos_ref, sin_ref, there)
        q = (dot_nn(x, wq) + bias[0:1]) * cosine + (dot_nn(x, wqt) + turned[0:1]) * sine
        k = (dot_nn(x, wk) + bias[1:2]) * cosine + (dot_nn(x, wkt) + turned[1:2]) * sine
        q_ref[there, :] = q.astype(BF)
        k_ref[there, :] = k.astype(BF)
        v_ref[there, :] = (dot_nn(x, wv) + bias[2:3]).astype(BF)
    for i in range(4):
        n = (i + 1) * 256
        rows = slice(i * 256, n)
        q, k, v = q_ref[rows, :], k_ref[:n, :], v_ref[:n, :]
        allowed = allowed_t(start_ref[:, rows], i, n)
        mixed = jnp.zeros((256, COLS), F32)
        for h in range(HEADS_HERE):
            mask = head_mask(h)
            scores = dot_nt(k, q * (mask * BF(0.125)))
            scores = jnp.where(allowed, scores, NEG_FILL)
            top = jnp.max(scores, 0, keepdims=True)
            shifted = jnp.exp(scores - top)
            total = jnp.sum(shifted, 0, keepdims=True)
            probability = (shifted * (1.0 / total)).astype(BF)
            mixed = mixed + dot_tn(probability, v) * mask.astype(F32)
            lse_ref[h : h + 1, rows] = top + jnp.log(total)
        there = pl.ds(pl.multiple_of((me ^ i) * 256, 256), 256)
        mixed_ref[there, :] = mixed.astype(BF)


def attend_forward(me, first, w, bias, turn, cosine, sine, start):
    whole = pl.BlockSpec(memory_space=VMEM)
    ins = (me, *first, w, bias, turn, cosine, sine, start)
    outs = [((1024, COLS), BF)] * 3 + [((8, 1024), F32), ((1024, COLS), BF)]
    return call(
        attend_forward_kernel, outs, ins, in_specs=[SMEM_SPEC] + [whole] * 4 + [NEAR_SPEC] + [whole] * 5,
        grid=(1,), flops=10**7,
    )


def gelu_and_slope(pre):
    below = 0.5 * (1.0 + lax.erf(pre * 0.7071067811865476))
    return pre * below, below + pre * jnp.exp(-0.5 * pre * pre) * 0.3989422804014327


def forward_out_kernel(keep_in_ref, send_in_ref, mixed_ref, rest_ref, bias_ref, hidden_ref, slope_ref, keep_ref, send_ref):
    up_bias = jnp.concatenate([bias_ref[3 + r : 4 + r, :] for r in range(4)], 1)
    for a in range(2):
        rows = slice(a * 256, (a + 1) * 256)
        pre = dot_nn((keep_in_ref, send_in_ref)[a][...], rest_ref[:, :D]) + up_bias
        hidden, slope = gelu_and_slope(pre)
        hidden = hidden.astype(BF)
        hidden_ref[rows, :] = hidden
        slope_ref[rows, :] = slope
        out = dot_nt(hidden, rest_ref[:, D : 2 * D]) + dot_nt(mixed_ref[rows, :], rest_ref[:, 2 * D : 2 * D + COLS])
        if a == 0:
            keep_ref[...] = out
        else:
            send_ref[...] = out.astype(BF)


def forward_out(second, mixed, rest, bias, half):
    part = lambda n: pl.BlockSpec((512, n), lambda i, half=half: (half, 0))
    full = lambda *s: pl.BlockSpec(s, lambda i: (0,) * len(s))
    return pl.pallas_call(
        forward_out_kernel,
        grid=(1,),
        out_shape=[jax.ShapeDtypeStruct(s, d) for s, d in (((512, D), BF), ((512, D), F32), ((256, D), F32), ((256, D), BF))],
        in_specs=[full(256, D), full(256, D), part(COLS), full(D, WIDE), full(7, COLS)],
        out_specs=[full(512, D), full(512, D), full(256, D), full(256, D)],
        compiler_params=pltpu.CompilerParams(vmem_limit_bytes=60 << 20),
        cost_estimate=pl.CostEstimate(flops=10**7, bytes_accessed=1 << 16, transcendentals=0),
    )(second[2 * half], second[2 * half + 1], mixed, rest, bias)


def backward_rest_kernel(*refs):
    slots, refs = refs[:12], refs[12:]
    hidden_ref, hidden_far_ref, mixed_ref, slope_ref, slope_far_ref, rest_ref, gain_ref = refs[:7]
    grad_ref, d_mixed_ref, w_ref, sums_ref, acc_ref = refs[7:]
    step = pl.program_id(0)

    def one(slot):
        outer, second, scaled = slots[slot][...], slots[4 + slot][...], slots[8 + slot][...]
        hidden = (hidden_ref if slot < 2 else hidden_far_ref)[...]
        slope = (slope_ref if slot < 2 else slope_far_ref)[...]
        d_hidden = dot_nn(outer, rest_ref[:, D : 2 * D])
        d_mixed_ref[...] = dot_nn(outer, rest_ref[:, 2 * D : 2 * D + COLS]).astype(BF)
        d_pre = (d_hidden * slope).astype(BF)
        d_second = dot_nt(d_pre, rest_ref[:, :D])
        w_ref[...] = d_second * gain_ref[2:3, :]
        sums = jnp.concatenate(
            [
                jnp.sum(d_second * scaled.astype(F32), 0, keepdims=True),
                jnp.sum(d_second, 0, keepdims=True),
                jnp.sum(d_pre.astype(F32), 0, keepdims=True),
                jnp.zeros((5, D), F32),
            ],
            0,
        )
        up, down, out = dot_tn(second, d_pre), dot_tn(outer, hidden), dot_tn(outer, mixed_ref[...])
        if slot == 0:
            acc_ref[:, :D] = up
            acc_ref[:, D : 2 * D] = down
            acc_ref[:, 2 * D :] = out
            sums_ref[...] = sums
        elif slot < 3:
            acc_ref[:, :D] += up
            acc_ref[:, D : 2 * D] += down
            acc_ref[:, 2 * D :] += out
            sums_ref[...] += sums
        else:
            for total, first, last in ((up, 0, D), (down, D, 2 * D), (out, 2 * D, 1728)):
                total = acc_ref[:, first:last] + total
                for x in range(2):
                    for plane in range(16):
                        row = x * 384 + plane * CHUNK
                        grad_ref[plane, x, :, first:last] = total[row : row + CHUNK].astype(BF)
            sums_ref[...] += sums

    for slot in range(4):
        pl.when(step == slot)(lambda slot=slot: one(slot))


def backward_rest(outer, second, scaled, hidden, hidden_far, mixed, slope, slope_far, rest, gain):
    part = lambda n: pl.BlockSpec((256, n), lambda i: (i, 0))
    early = lambda n: pl.BlockSpec((256, n), lambda i: (jnp.minimum(i, 1), 0))
    late = lambda n: pl.BlockSpec((256, n), lambda i: (jnp.maximum(i, 2) - 2, 0))
    full = lambda *s: pl.BlockSpec(s, lambda i: (0,) * len(s))
    return pl.pallas_call(
        backward_rest_kernel,
        grid=(4,),
        out_shape=[
            jax.ShapeDtypeStruct(s, d)
            for s, d in (((16, 2, CHUNK, 1728), BF), ((1024, COLS), BF), ((1024, D), F32), ((8, D), F32))
        ],
        in_specs=[full(256, D)] * 12 + [early(D), late(D), part(COLS), early(D), late(D), full(D, WIDE), full(6, D)],
        out_specs=[full(16, 2, CHUNK, 1728), part(COLS), part(D), full(8, D)],
        scratch_shapes=[pltpu.VMEM((D, 1728), F32)],
        compiler_params=pltpu.CompilerParams(vmem_limit_bytes=60 << 20),
        cost_estimate=pl.CostEstimate(flops=10**7, bytes_accessed=1 << 16, transcendentals=0),
    )(*outer, *second, *scaled, hidden, hidden_far, mixed, slope, slope_far, rest, gain)


def attend_backward_kernel(
    me_ref, q_ref, k_ref, v_ref, lse_ref, d_mixed_ref, start_ref, cos_ref, sin_ref, turn_ref,
    w_ref, gain_ref, scaled0_ref, scaled1_ref, scaled2_ref, scaled3_ref, part_ref,
    proj_ref, keep_ref, send_ref, sums_ref, bias_ref, dq_ref, dk_ref, dv_ref,
):
    me = me_ref[0]
    dk_ref[...] = jnp.zeros((1024, COLS), F32)
    dv_ref[...] = jnp.zeros((1024, COLS), F32)
    for i in range(4):
        n = (i + 1) * 256
        rows = slice(i * 256, n)
        there = pl.ds(pl.multiple_of((me ^ i) * 256, 256), 256)
        d_mixed = d_mixed_ref[there, :]
        q, k, v = q_ref[rows, :], k_ref[:n, :], v_ref[:n, :]
        allowed = allowed_t(start_ref[:, rows], i, n)
        dq = jnp.zeros((256, COLS), F32)
        for h in range(HEADS_HERE):
            mask = head_mask(h)
            q_here = q * (mask * BF(0.125))
            d_here = d_mixed * mask
            scores = dot_nt(k, q_here)
            probability = jnp.where(allowed, jnp.exp(scores - lse_ref[h : h + 1, rows]), 0.0)
            d_prob = dot_nt(v, d_here)
            row = jnp.sum(probability * d_prob, 0, keepdims=True)
            d_score = (probability * (d_prob - row)).astype(BF)
            dq = dq + dot_tn(d_score, k) * (mask.astype(F32) * 0.125)
            dk_ref[:n, :] += dot_nn(d_score, q_here)
            dv_ref[:n, :] += dot_nn(probability.astype(BF), d_here)
        dq_ref[rows, :] = dq
    turn = turn_ref[...]

    def back(value, cosine, sine):
        upper = value.astype(BF)
        lower = (value - upper.astype(F32)).astype(BF)
        return value * cosine - (dot_nn(upper, turn) + dot_nn(lower, turn)) * sine

    sums = jnp.zeros((8, D), F32)
    bias = jnp.zeros((8, 576), F32)
    for a in range(4):
        there = pl.ds(pl.multiple_of((me ^ a) * 256, 256), 256)
        rows = slice(a * 256, (a + 1) * 256)
        cosine, sine = rope_at(cos_ref, sin_ref, there)
        dq = back(dq_ref[there, :], cosine, sine)
        dk = back(dk_ref[there, :], cosine, sine)
        proj = jnp.concatenate([dq, dk, dv_ref[there, :]], 1).astype(BF)
        proj_ref[rows, :] = proj
        d_first = dot_nt(proj, w_ref[:, COLS:])
        scaled = (scaled0_ref, scaled1_ref, scaled2_ref, scaled3_ref)[a][...]
        weighted = d_first * gain_ref[0:1, :] + part_ref[rows, :]
        if a % 2 == 0:
            keep_ref[a // 2] = weighted
        else:
            send_ref[a // 2] = weighted.astype(BF)
        sums = sums + jnp.concatenate(
            [
                jnp.sum(d_first * scaled.astype(F32), 0, keepdims=True),
                jnp.sum(d_first, 0, keepdims=True),
                jnp.zeros((6, D), F32),
            ],
            0,
        )
        bias = bias + jnp.concatenate(
            [jnp.sum(proj.astype(F32), 0, keepdims=True), jnp.zeros((7, 576), F32)], 0
        )
    sums_ref[...] = sums
    bias_ref[...] = bias


def attend_backward(me, q, k, v, lse, d_mixed, start, cosine, sine, turn, w, gain, scaled, part):
    whole = pl.BlockSpec(memory_space=VMEM)
    ins = (me, q, k, v, lse, d_mixed, start, cosine, sine, turn, w, gain, *scaled, part)
    outs = [((1024, 576), BF), ((2, 256, D), F32), ((2, 256, D), BF), ((8, D), F32), ((8, 576), F32)]
    return call(
        attend_backward_kernel, outs, ins, in_specs=[SMEM_SPEC] + [whole] * 9 + [NEAR_SPEC] + [whole] * 6,
        grid=(1,), scratch=[pltpu.VMEM((1024, COLS), F32)] * 3, flops=10**7,
    )


def grad_near_kernel(
    direct, first0_ref, first1_ref, first2_ref, first3_ref, proj_ref, sums_ref, sums_rest_ref, bias_ref, upstream_ref, out_ref
):
    total = dot_tn(first0_ref[...], proj_ref[:256, :])
    for a, ref in ((1, first1_ref), (2, first2_ref), (3, first3_ref)):
        total = total + dot_tn(ref[...], proj_ref[a * 256 : (a + 1) * 256, :])
    pre = sums_rest_ref[2:3, :]
    upper, lower = split(
        jnp.concatenate(
            [
                sums_ref[:2, :],
                sums_rest_ref[:2, :],
                jnp.sum(upstream_ref[...], 0, keepdims=True),
                jnp.concatenate([bias_ref[:1, :], pre[:, :COLS]], 1),
                jnp.concatenate([pre[:, COLS:], jnp.zeros((1, COLS), F32)], 1),
                jnp.zeros((1, D), F32),
            ],
            0,
        )
    )
    row = lax.broadcasted_iota(jnp.int32, (8, 16), 0)
    lane = lax.broadcasted_iota(jnp.int32, (8, 16), 1)
    small = dot_tn(upper, (row == lane).astype(BF)) + dot_tn(lower, (row + 8 == lane).astype(BF))
    for x in range(2):
        for plane in range(16):
            here = slice(x * 384 + plane * CHUNK, x * 384 + (plane + 1) * CHUNK)
            place = (x * 16 + plane,) if direct else (plane, x)
            out_ref[(*place, slice(None), slice(0, 576))] = total[here].astype(BF)
            out_ref[(*place, slice(None), slice(576, 592))] = small[here].astype(BF)


def grad_near(first, proj, parts, direct):
    shape = (32, CHUNK, 592) if direct else (16, 2, CHUNK, 592)
    return call(functools.partial(grad_near_kernel, direct), [(shape, BF)], (*first, proj, *parts), flops=10**7)[0]


def split(value):
    upper = value.astype(BF)
    return upper, (value - upper.astype(F32)).astype(BF)


def newton_schulz_kernel(
    place_ref, p0, p1, p2, p3, q0, q1, q2, q3, small_ref, out_ref,
    m_ref, g_ref, h_ref, gs_ref, ss_ref, hs_ref, x_ref, xs_ref,
):
    x, y = place_ref[0], place_ref[1]
    lane = lax.broadcasted_iota(jnp.int32, (1, D), 1)
    half = y // 2
    used = (x == 0) | ((lane >= half * COLS) & (lane < (half + 1) * COLS))
    for s, (p, q) in enumerate(((p0, q0), (p1, q1), (p2, q2), (p3, q3))):
        for b, ref in enumerate((p, q)):
            for c in range(2):
                m_ref[2 * b + c, s * 192 : (s + 1) * 192, :] = jnp.where(used, ref[c], jnp.zeros((), BF))

    def store(pair, lower, i, j, value):
        r, c = slice(i * 256, (i + 1) * 256), slice(j * 256, (j + 1) * 256)
        upper_part, lower_part = split(value)
        pair[0, r, c] = upper_part
        pair[1, r, c] = lower_part
        if i != j and lower:
            upper_part, lower_part = split(value.T)
            pair[0, c, r] = upper_part
            pair[1, c, r] = lower_part

    def product(a, b, finish):
        for j in range(3):
            n, c = (j + 1) * 256, slice(j * 256, (j + 1) * 256)
            value = dot_nn(a[0, :n, :], b[0, :, c]) + dot_nn(a[0, :n, :], b[1, :, c]) + dot_nn(a[1, :n, :], b[0, :, c])
            for i in range(j + 1):
                finish(i, j, value[i * 256 : (i + 1) * 256])

    def at(ref, i, j):
        return ref[i * 256 : (i + 1) * 256, j * 256 : (j + 1) * 256]

    def put(ref, i, j, value):
        ref[i * 256 : (i + 1) * 256, j * 256 : (j + 1) * 256] = value

    for j in range(3):
        n, c = (j + 1) * 256, slice(j * 256, (j + 1) * 256)
        value = dot_nt(m_ref[0, :n, :], m_ref[0, c, :])
        for b in range(1, 4):
            value = value + dot_nt(m_ref[b, :n, :], m_ref[b, c, :])
        g_ref[:n, c] = value
    trace = jnp.zeros((1, 1), F32)
    same = lax.broadcasted_iota(jnp.int32, (256, 256), 0) == lax.broadcasted_iota(jnp.int32, (256, 256), 1)
    for i in range(3):
        diagonal = jnp.where(same, at(g_ref, i, i), 0.0)
        trace = trace + jnp.sum(jnp.sum(diagonal, 1, keepdims=True), 0, keepdims=True)
    scale = 1.0 / (jnp.sqrt(trace) + EPS_ORTH)
    for j in range(3):
        for i in range(j + 1):
            value = at(g_ref, i, j) * (scale * scale)
            put(g_ref, i, j, value)
            store(gs_ref, True, i, j, value)
    which = jnp.where(x == 0, y, half)
    block = jnp.zeros((D, COLS), BF)
    for i in range(4):
        block = jnp.where(which == i, m_ref[0, :, i * COLS : (i + 1) * COLS], block)
    current = block.astype(F32) * scale
    x_ref[...] = current
    xs_ref[0], xs_ref[1] = split(current)

    def mix():
        def finish(i, j, value):
            store(ss_ref, True, i, j, COEF_B * at(g_ref, i, j) + COEF_C * value)

        product(gs_ref, gs_ref, finish)

    def advance():
        s0, s1 = ss_ref[0], ss_ref[1]
        return COEF_A * x_ref[...] + dot_nn(s0, xs_ref[0]) + dot_nn(s0, xs_ref[1]) + dot_nn(s1, xs_ref[0])

    def step(_, carry):
        mix()
        current = advance()
        x_ref[...] = current
        xs_ref[0], xs_ref[1] = split(current)

        def finish_h(i, j, value):
            value = COEF_A * at(g_ref, i, j) + value
            put(h_ref, i, j, value)
            store(hs_ref, True, i, j, value)

        product(ss_ref, gs_ref, finish_h)

        def finish_g(i, j, value):
            value = COEF_A * at(h_ref, i, j) + value
            put(g_ref, i, j, value)
            store(gs_ref, True, i, j, value)

        product(hs_ref, ss_ref, finish_g)
        return carry

    lax.fori_loop(0, NS_STEPS - 1, step, 0)
    mix()
    current = advance()
    for s in range(4):
        for group in range(8):
            row = s * 192 + group * 24
            out_ref[group, y ^ s, :, :COLS] = current[row : row + 24].astype(BF)
            out_ref[group, y ^ s, :, COLS:] = small_ref[...]


def newton_schulz(place, pieces, small):
    pair = pltpu.VMEM((2, D, D), BF)
    whole = pl.BlockSpec(memory_space=VMEM)
    return call(
        newton_schulz_kernel, [((8, 4, CHUNK, 224), BF)], (place, *pieces, small),
        in_specs=[SMEM_SPEC] + [whole] * 9,
        scratch=[pltpu.VMEM((4, D, D), BF)] + [pltpu.VMEM((D, D), F32)] * 2 + [pair] * 3
        + [pltpu.VMEM((D, COLS), F32), pltpu.VMEM((2, D, COLS), BF)],
        flops=10**7,
    )[0]


def pack_kernel(attn_ref, mlp_ref, out_ref):
    for layer in range(2):
        for m in range(2):
            parts = [mlp_ref[layer, m, :, r, :] for r in range(4)]
            out_ref[layer, :, m * D : (m + 1) * D] = jnp.concatenate(parts, 1).astype(BF)
        parts = [attn_ref[layer, m] for m in (3, 0, 1, 2)]
        out_ref[layer, :, 2 * D :] = jnp.concatenate(parts, 1).astype(BF)


def pack(attn_w, mlp_w):
    return call(pack_kernel, [((2, CHUNK, WIDE), BF)], (attn_w, mlp_w))[0]


def assemble_kernel(place_ref, a0, a1, a2, a2_more, a3, b0, b1, b2, b2_more, b3, out_ref):
    x, z, y = place_ref[0], place_ref[1], place_ref[2]
    for other, blocks in enumerate(((a0, a1, (a2, a2_more), a3), (b0, b1, (b2, b2_more), b3))):
        for outer, block in enumerate(blocks):
            for inner in range(4):
                value = block[inner // 2][inner % 2] if outer == 2 else block[inner]
                zr, yr = (outer, inner) if other else (inner, outer)
                out_ref[(x ^ other) * 16 + (z ^ zr) * 4 + (y ^ yr)] = value


def assemble(place, blocks):
    whole = pl.BlockSpec(memory_space=VMEM)
    return call(
        assemble_kernel, [((32, CHUNK, WIDE), BF)], (place, *blocks), in_specs=[SMEM_SPEC] + [whole] * 10
    )[0]


def momenta_kernel(
    attn_ref, mlp_ref, rest0_ref, rest1_ref, near1_ref, near0_ref, new_attn_ref, new_mlp_ref, sends_ref, small_ref
):
    total = jnp.sum(near0_ref[...].astype(F32), 0)
    near1 = near1_ref[...]
    none = jnp.zeros((CHUNK, 2 * COLS), BF)
    for layer, rest_ref, near in ((0, rest0_ref, total), (1, rest1_ref, near1)):
        for m in range(2):
            parts = []
            for r in range(4):
                first = m * D + r * COLS
                mom = MOMENTUM * mlp_ref[layer, m, :, r, :] + rest_ref[:, first : first + COLS]
                new_mlp_ref[layer, m, :, r, :] = mom
                parts.append(mom.astype(BF))
            sends_ref[2 * layer + m] = jnp.concatenate(parts, 1)
        parts = []
        for m in range(4):
            grad = near[:, m * COLS : (m + 1) * COLS] if m < 3 else rest_ref[:, 2 * D :]
            mom = MOMENTUM * attn_ref[layer, m] + grad
            new_attn_ref[layer, m] = mom
            parts.append(mom.astype(BF))
        sends_ref[4 + 2 * layer] = jnp.concatenate([*parts[:2], none], 1)
        sends_ref[5 + 2 * layer] = jnp.concatenate([*parts[2:], none], 1)
    here = total[:, 576:583] + total[:, 584:591]
    last = near1[:, 576:583] + near1[:, 584:591]
    small_ref[...] = jnp.concatenate([here[:, :5], last[:, :5], here[:, 5:], last[:, 5:]], 1)


def momenta(mom_attn, mom_mlp, *ins):
    outs = [(mom_attn.shape, F32), (mom_mlp.shape, F32), ((8, CHUNK, D), BF), ((CHUNK, 14), F32)]
    return call(momenta_kernel, outs, (mom_attn, mom_mlp, *ins))


def new_weights_kernel(back_ref, attn_ref, mlp_ref, new_attn_ref, new_mlp_ref, small_ref):
    def block(x, z, y):
        return back_ref[x * 16 + z * 4 + y, :, :COLS].astype(F32)

    for layer in range(2):
        for m in range(4):
            step = STEP_SCALE * math.sqrt(D) * block(1, 2 * layer + m // 2, 2 * (m % 2))
            new_attn_ref[layer, m] = attn_ref[layer, m] - step
        for m in range(2):
            for r in range(4):
                step = STEP_SCALE * math.sqrt(FF) * block(0, 2 * layer + m, r)
                new_mlp_ref[layer, m, :, r, :] = mlp_ref[layer, m, :, r, :] - step
    for i in range(32):
        part = back_ref[i, :, COLS:].astype(F32)
        small_ref[i] = part[:, :14] + part[:, 14:28]


def new_weights(back, attn_w, mlp_w):
    outs = [(attn_w.shape, F32), (mlp_w.shape, F32), ((32, CHUNK, 14), F32)]
    attn, mlp, small = call(new_weights_kernel, outs, (back, attn_w, mlp_w))
    return attn, mlp, small.reshape(D, 14)


def dp_swap(value, mask):
    return lax.ppermute(value, "dp", [(i, i ^ mask) for i in range(32)])


def tensor_swap(value, mask):
    return lax.ppermute(value, "tensor", [(i, i ^ mask) for i in range(4)])


def dp_place():
    me = lax.axis_index("dp")
    return me // 16, (me // 4) % 4, me % 4


def swap_four(pieces, unit):
    return [pieces[0]] + [dp_swap(pieces[s], s * unit) for s in (1, 2, 3)]


PLANE = [[x * 16 + i for i in range(16)] for x in range(2)]


def by_x(own, other):
    x = dp_place()[0]
    return jnp.stack([jnp.where(x == 0, own, other), jnp.where(x == 0, other, own)])


def spread_rows(shard, other):
    return jnp.concatenate([by_x(shard, other)[None]] * 16, 0)


def gather_rows(spread):
    return lax.all_to_all(spread, "dp", 0, 0, tiled=True, axis_index_groups=PLANE)


def gather_by_rings(shard):
    x, z, y = dp_place()
    other = dp_swap(shard, 16)
    halves = []
    for mine, unit, then in ((shard, 4, 1), (other, 1, 4)):
        block = jnp.stack(swap_four([mine] * 4, unit))
        left, right = dp_swap(block, then), dp_swap(block, 3 * then)
        halves += [block, left, dp_swap(right[:2], then), dp_swap(left[2:], 3 * then), right]
    return assemble(jnp.stack([x, z, y]).astype(jnp.int32), halves).reshape(D, WIDE)


def in_order(arrived):
    return arrived.transpose(1, 0, 2, 3).reshape(D, arrived.shape[3])


def scatter_rows(partial):
    return lax.all_to_all(partial, "dp", 0, 0, tiled=True, axis_index_groups=PLANE)


def add_arrived(arrived):
    sums = jnp.sum(arrived.astype(F32), 0)
    x = dp_place()[0]
    other = jnp.where(x == 0, sums[1], sums[0]).astype(BF)
    return jnp.where(x == 0, sums[0], sums[1]) + dp_swap(other, 16).astype(F32)


def gather_tokens(mine, beside=None):
    far = tensor_swap(mine, 2)
    near = tensor_swap(mine, 1)
    if beside is not None:
        far, beside = lax.optimization_barrier((far, beside))
    return [mine, near, far, tensor_swap(far, 1)], beside


def standardize(stream):
    center = stream - jnp.mean(stream, -1, keepdims=True)
    inverse = lax.rsqrt(jnp.mean(center * center, -1, keepdims=True) + EPS_NORM)
    return center * inverse, inverse


def rope_tables(labels):
    kinds = jnp.arange(8, dtype=jnp.int32)
    below = jnp.sum((labels[None, :] < kinds[:, None]).astype(jnp.int32), 1)
    start = jnp.sum(jnp.where(labels[None, :] == kinds[:, None], below[:, None], 0), 0)
    places = jnp.arange(labels.shape[0], dtype=jnp.int32) - start
    frequency = 10000.0 ** (jnp.arange(ROT // 2, dtype=F32) * (-2.0 / ROT))
    angles = places.astype(F32)[None, :] * frequency[:, None]
    cosine, sine = jnp.cos(angles), jnp.sin(angles)
    return jnp.cos(angles), jnp.sin(angles), start[None, :]


def turn_matrix():
    turn = np.zeros((COLS, COLS), np.float32)
    for head in range(HEADS_HERE):
        for i in range(ROT // 2):
            turn[head * HD + i + ROT // 2, head * HD + i] = -1.0
            turn[head * HD + i, head * HD + i + ROT // 2] = 1.0
    return turn


def normalized(stream, vector_rows, beside=None):
    scaled, inverse = standardize(stream)
    first, second, scaled_all = [], [], []
    slots, beside = gather_tokens(scaled.astype(jnp.float16), beside)
    for slot in slots:
        wide = slot.astype(F32)
        first.append((wide * vector_rows[0] + vector_rows[1]).astype(BF))
        second.append((wide * vector_rows[2] + vector_rows[3]).astype(BF))
        scaled_all.append(wide.astype(BF))
    return (scaled, inverse, first, second, scaled_all), beside


def forward_layer(stream, norms, weights, bias_rows, vector_rows, common):
    me, cosine, sine, start, turn = common
    scaled, inverse, first, second, scaled_all = norms
    q, k, v, lse, mixed = attend_forward(
        me, first, weights, bias_rows, turn, cosine, sine, start
    )
    hidden_far, slope_far, keep_far, send_far = forward_out(second, mixed, weights, bias_rows, 1)
    pair = (keep_far + tensor_swap(send_far, 1).astype(F32)).astype(BF)
    mixed, pair = lax.optimization_barrier((mixed, pair))
    hidden, slope, keep, send = forward_out(second, mixed, weights, bias_rows, 0)
    branch = keep + tensor_swap(send, 1).astype(F32) + tensor_swap(pair, 2).astype(F32)
    record = (q, k, v, lse, mixed, hidden, hidden_far, slope, slope_far)
    return record, stream + branch + vector_rows[4] + vector_rows[5]


def backward_layer(upstream, outer, record, weights, vector_rows, common, ready, last):
    me, cosine, sine, start, turn = common
    scaled, inverse, first, second, scaled_all, q, k, v, lse, mixed, hidden, hidden_far, slope, slope_far = record
    grad_rest, d_mixed, part, sums_rest = backward_rest(
        outer, second, scaled_all, hidden, hidden_far, mixed, slope, slope_far, weights, vector_rows
    )
    grad_rest = scatter_rows(grad_rest)
    d_mixed, ready = lax.optimization_barrier((d_mixed, ready))
    proj, keep, send, sums, bias = attend_backward(
        me, q, k, v, lse, d_mixed, start, cosine, sine, turn, weights, vector_rows, scaled_all, part
    )
    pair = keep + tensor_swap(send, 1).astype(F32)
    weighted = pair[0] + tensor_swap(pair[1].astype(BF), 2).astype(F32)
    new_upstream = upstream + inverse * (
        weighted
        - jnp.mean(weighted, -1, keepdims=True)
        - scaled * jnp.mean(weighted * scaled, -1, keepdims=True)
    )
    grad_near_here, grad_rest = lax.optimization_barrier((grad_near(first, proj, (sums, sums_rest, bias, upstream), last), grad_rest))
    grad_near_here = (
        lax.all_to_all(grad_near_here, "dp", 0, 0, tiled=True) if last else scatter_rows(grad_near_here)
    )
    return new_upstream, grad_rest, grad_near_here, ready


def two_terms(value):
    upper = value.astype(BF)
    return jnp.concatenate([upper, (value - upper.astype(F32)).astype(BF)], 1)


def orthogonal_blocks(sends, small):
    x, z, y = dp_place()
    groups = [[i + y_place for i in range(0, 32, 4)] for y_place in range(4)]
    rows = lax.all_to_all(sends, "dp", 0, 0, tiled=True, axis_index_groups=groups).reshape(192, D)
    shared = small[:, :10]
    shared = shared + tensor_swap(shared, 1)
    shared = shared + tensor_swap(shared, 2)
    pieces = swap_four([jnp.stack([rows, tensor_swap(rows, 2)])] * 4, 1)
    pieces[1], shared = lax.optimization_barrier((pieces[1], shared))
    pieces = pieces + [tensor_swap(piece, 1) for piece in pieces]
    small = two_terms(jnp.concatenate([shared, small[:, 10:]], 1))
    small = jnp.pad(small, ((0, 0), (0, 4)))
    result = newton_schulz(jnp.stack([x, y]).astype(jnp.int32), pieces, small)
    return lax.all_to_all(result.reshape(32, CHUNK, 224), "dp", 0, 0, tiled=True)


def per_device(
    x_in, segments, attn_w, mlp_w, in_bias, vectors, mom_attn, mom_mlp, mom_bias, mom_vec, cotangent
):
    cosine, sine, start = rope_tables(segments[0])
    me = lax.axis_index("tensor").astype(jnp.int32).reshape(1)
    common = (me, cosine, sine, start, jnp.asarray(turn_matrix(), BF))
    shards = pack(attn_w, mlp_w)
    arrived = gather_by_rings(shards[0])
    later = spread_rows(shards[1], dp_swap(shards[1], 16))
    stream = x_in[0].astype(F32)
    upstream = cotangent[0]
    norms, _ = normalized(stream, vectors[0])
    arrived, later, norms, common = lax.optimization_barrier((arrived, later, norms, common))
    weights = [arrived]
    arrived = gather_rows(later)
    record, stream = forward_layer(stream, norms, weights[0], in_bias[0], vectors[0], common)
    saved = [norms + record]
    stream, arrived = lax.optimization_barrier((stream, arrived))
    norms, last = normalized(stream, vectors[1], in_order(arrived))
    weights.append(last)
    record, stream = forward_layer(stream, norms, weights[1], in_bias[1], vectors[1], common)
    saved.append(norms + record)
    rests, nears = [None, None], [None, None]
    outer, _ = gather_tokens(upstream.astype(BF))
    upstream, rests[1], nears[1], stream = backward_layer(
        upstream, outer, saved[1], weights[1], vectors[1], common, stream, False
    )
    outer, _ = gather_tokens(upstream.astype(BF))
    upstream, rests[0], nears[0], nears[1] = backward_layer(
        upstream, outer, saved[0], weights[0], vectors[0], common, nears[1], True
    )
    rests, last_near = [add_arrived(rest) for rest in rests], add_arrived(nears[1])
    new_mom_attn, new_mom_mlp, sends, small = momenta(mom_attn, mom_mlp, rests[0], rests[1], last_near, nears[0])
    result = orthogonal_blocks(sends, small)
    new_attn_w, new_mlp_w, small = new_weights(result, attn_w, mlp_w)
    vec_total = small[:, :10].T.reshape(2, 5, D)
    vec_total = jnp.concatenate([vec_total, vec_total[:, 4:]], 1)
    bias_total = small[:, 10:].T.reshape(2, 2 * D)[:, :1344].reshape(2, 7, COLS)
    new_mom_bias = MOMENTUM * mom_bias + bias_total
    new_mom_vec = MOMENTUM * mom_vec + vec_total
    vec_rate = RATE_VEC / math.sqrt(32768)
    return (
        stream[None],
        upstream[None],
        new_mom_attn,
        new_attn_w,
        new_mom_mlp,
        new_mlp_w,
        new_mom_bias,
        in_bias - vec_rate * new_mom_bias,
        new_mom_vec,
        vectors - vec_rate * new_mom_vec,
    )


def solution(mesh):
    placed = (
        P("dp", "tensor", None),
        P("dp", None),
        P(None, None, "dp", "tensor"),
        P(None, None, "dp", None, "tensor"),
        P(None, None, "tensor"),
        P(),
        P(None, None, "dp", "tensor"),
        P(None, None, "dp", None, "tensor"),
        P(None, None, "tensor"),
        P(),
        P("dp", "tensor", None),
    )
    return jax.shard_map(
        per_device,
        mesh=mesh,
        in_specs=placed,
        out_specs=(
            P("dp", "tensor", None),
            P("dp", "tensor", None),
            P(None, None, "dp", "tensor"),
            P(None, None, "dp", "tensor"),
            P(None, None, "dp", None, "tensor"),
            P(None, None, "dp", None, "tensor"),
            P(None, None, "tensor"),
            P(None, None, "tensor"),
            P(),
            P(),
        ),
        check_vma=False,
    )
```

```python
import functools
import math

import jax
import jax.numpy as jnp
import numpy as np
from jax import lax
from jax.experimental import pallas as pl
from jax.experimental.pallas import tpu as pltpu
from jax.sharding import PartitionSpec as P

D = 768
FF = 3072
HD = 64
ROT = 16
CHUNK = 24
EPS_NORM = 1e-05
MOMENTUM = 0.95
STEP_SCALE = 0.4
RATE_VEC = 0.5
COLS = 192
HEADS_HERE = 3
NS_STEPS = 5
EPS_ORTH = 1e-07
COEF_A = 3.4445
COEF_B = -4.775
COEF_C = 2.0315
NEG_FILL = -1e30
F1_LIMIT, F2_LIMIT, B1_LIMIT, B2_LIMIT, GN_LIMIT, NS_LIMIT, OTHER_LIMIT = 10, 6, 14, 14, 8, 26, 6
BF = jnp.bfloat16
F32 = jnp.float32
VMEM = pltpu.VMEM


def dot_nn(a, b):
    return lax.dot_general(a, b, (((1,), (0,)), ((), ())), preferred_element_type=F32)


def dot_nt(a, b):
    return lax.dot_general(a, b, (((1,), (1,)), ((), ())), preferred_element_type=F32)


def dot_tn(a, b):
    return lax.dot_general(a, b, (((0,), (0,)), ((), ())), preferred_element_type=F32)


def call(kernel, outs, ins, scratch=(), grid=None, in_specs=None, out_specs=None, flops=0, limit=OTHER_LIMIT):
    whole = pl.BlockSpec(memory_space=VMEM)
    kwargs = {} if grid is None else dict(grid=grid)
    return pl.pallas_call(
        kernel,
        out_shape=[jax.ShapeDtypeStruct(s, d) for s, d in outs],
        in_specs=in_specs or [whole] * len(ins),
        out_specs=out_specs or [whole] * len(outs),
        scratch_shapes=list(scratch),
        compiler_params=pltpu.CompilerParams(vmem_limit_bytes=limit * 1024 * 1024),
        cost_estimate=pl.CostEstimate(flops=flops, bytes_accessed=1 << 16, transcendentals=0),
        **kwargs,
    )(*ins)


SMEM_SPEC = pl.BlockSpec(memory_space=pltpu.SMEM)
WIDE = 2304


def head_mask(h):
    lane = lax.broadcasted_iota(jnp.int32, (1, COLS), 1)
    return ((lane >= h * HD) & (lane < (h + 1) * HD)).astype(BF)


def allowed_t(start_row, i, width):
    key = lax.broadcasted_iota(jnp.int32, (width, 256), 0)
    query = lax.broadcasted_iota(jnp.int32, (width, 256), 1) + i * 256
    return (key >= start_row) & (key <= query)


def by_heads(rows):
    return jnp.concatenate([rows * head_mask(h) for h in range(HEADS_HERE)], 0)


def own_lanes(stacked):
    return sum(stacked[h * 256 : (h + 1) * 256] * head_mask(h).astype(F32) for h in range(HEADS_HERE))


def blocked(start_row, i, width):
    key = lax.broadcasted_iota(jnp.int32, (width, 256), 0)
    query = lax.broadcasted_iota(jnp.int32, (width, 256), 1) + i * 256
    once = jnp.where((key >= start_row) & (key <= query), 0.0, NEG_FILL)
    return jnp.concatenate([once] * HEADS_HERE, 1)


def rope_at(cos_ref, sin_ref, there):
    lane = lax.broadcasted_iota(jnp.int32, (8, COLS), 1) % HD
    angle = lax.broadcasted_iota(jnp.int32, (8, COLS), 0)
    spread = ((lane < ROT) & (lane % (ROT // 2) == angle)).astype(F32)
    rest = (lax.broadcasted_iota(jnp.int32, (1, COLS), 1) % HD >= ROT).astype(F32)
    exact = dict(preferred_element_type=F32, precision=lax.Precision.HIGHEST)
    over = (((0,), (0,)), ((), ()))
    cosine = lax.dot_general(cos_ref[:, there], spread, over, **exact) + rest
    return cosine, lax.dot_general(sin_ref[:, there], spread, over, **exact)


def attend_forward_kernel(
    me_ref, first0_ref, first1_ref, first2_ref, first3_ref, w_ref, bias_ref, turn_ref, cos_ref, sin_ref, start_ref,
    q_ref, k_ref, v_ref, lse_ref, mixed_ref,
):
    me = me_ref[0]
    turn = turn_ref[...]
    wq, wk, wv = w_ref[:, 1728:1920], w_ref[:, 1920:2112], w_ref[:, 2112:]
    wqt = dot_nn(wq, turn).astype(BF)
    wkt = dot_nn(wk, turn).astype(BF)
    bias = bias_ref[:3]
    turned = lax.dot_general(
        bias[:2], turn.astype(F32), (((1,), (0,)), ((), ())),
        preferred_element_type=F32, precision=lax.Precision.HIGHEST,
    )
    for a in range(4):
        there = pl.ds(pl.multiple_of((me ^ a) * 256, 256), 256)
        x = (first0_ref, first1_ref, first2_ref, first3_ref)[a][...]
        cosine, sine = rope_at(cos_ref, sin_ref, there)
        q = (dot_nn(x, wq) + bias[0:1]) * cosine + (dot_nn(x, wqt) + turned[0:1]) * sine
        k = (dot_nn(x, wk) + bias[1:2]) * cosine + (dot_nn(x, wkt) + turned[1:2]) * sine
        q_ref[there, :] = q.astype(BF)
        k_ref[there, :] = k.astype(BF)
        v_ref[there, :] = (dot_nn(x, wv) + bias[2:3]).astype(BF)
    for i in range(4):
        n = (i + 1) * 256
        rows = slice(i * 256, n)
        q, k, v = q_ref[rows, :], k_ref[:n, :], v_ref[:n, :]
        allowed = allowed_t(start_ref[:, rows], i, n)
        mixed = jnp.zeros((256, COLS), F32)
        for h in range(HEADS_HERE):
            mask = head_mask(h)
            scores = dot_nt(k, q * (mask * BF(0.125)))
            scores = jnp.where(allowed, scores, NEG_FILL)
            top = jnp.max(scores, 0, keepdims=True)
            shifted = jnp.exp(scores - top)
            total = jnp.sum(shifted, 0, keepdims=True)
            probability = (shifted * (1.0 / total)).astype(BF)
            mixed = mixed + dot_tn(probability, v) * mask.astype(F32)
            lse_ref[h : h + 1, rows] = top + jnp.log(total)
        there = pl.ds(pl.multiple_of((me ^ i) * 256, 256), 256)
        mixed_ref[there, :] = mixed.astype(BF)


def attend_forward(me, first, w, bias, turn, cosine, sine, start):
    whole = pl.BlockSpec(memory_space=VMEM)
    ins = (me, *first, w, bias, turn, cosine, sine, start)
    outs = [((1024, COLS), BF)] * 3 + [((8, 1024), F32), ((1024, COLS), BF)]
    return call(
        attend_forward_kernel, outs, ins, in_specs=[SMEM_SPEC] + [whole] * 10,
        flops=10**7, limit=F1_LIMIT,
    )


def gelu_and_slope(pre):
    below = 0.5 * (1.0 + lax.erf(pre * 0.7071067811865476))
    return pre * below, below + pre * jnp.exp(-0.5 * pre * pre) * 0.3989422804014327


def up_bias(bias_ref):
    return jnp.concatenate([bias_ref[3 + r : 4 + r, :] for r in range(4)], 1)


def forward_out_kernel(half, keep_in_ref, send_in_ref, mixed_ref, rest_ref, bias_ref, keep_ref, send_ref):
    bias = up_bias(bias_ref)
    for a in range(2):
        pre = dot_nn((keep_in_ref, send_in_ref)[a][...], rest_ref[:, :D]) + bias
        hidden = gelu_and_slope(pre)[0].astype(BF)
        mixed = mixed_ref[(2 * half + a) * 256 : (2 * half + a + 1) * 256, :]
        out = dot_nt(hidden, rest_ref[:, D : 2 * D]) + dot_nt(mixed, rest_ref[:, 2 * D : 2 * D + COLS])
        if a == 0:
            keep_ref[...] = out
        else:
            send_ref[...] = out.astype(BF)


def forward_out(second, mixed, rest, bias, half):
    ins = (second[2 * half], second[2 * half + 1], mixed, rest, bias)
    return call(
        functools.partial(forward_out_kernel, half), [((256, D), F32), ((256, D), BF)], ins, flops=10**7, limit=F2_LIMIT
    )


def backward_rest_kernel(*refs):
    slots, refs = refs[:12], refs[12:]
    mixed_ref, rest_ref, gain_ref, bias_ref, grad_ref, d_mixed_ref, w_ref, sums_ref, acc_ref = refs
    bias = up_bias(bias_ref)
    for slot in range(4):
        rows = slice(slot * 256, (slot + 1) * 256)
        outer, second, scaled = slots[slot][...], slots[4 + slot][...], slots[8 + slot][...]
        hidden, slope = gelu_and_slope(dot_nn(second, rest_ref[:, :D]) + bias)
        d_hidden = dot_nn(outer, rest_ref[:, D : 2 * D])
        d_mixed_ref[rows, :] = dot_nn(outer, rest_ref[:, 2 * D : 2 * D + COLS]).astype(BF)
        d_pre = (d_hidden * slope).astype(BF)
        d_second = dot_nt(d_pre, rest_ref[:, :D])
        w_ref[rows, :] = (d_second * gain_ref[2:3, :]).astype(BF)
        sums = jnp.concatenate(
            [
                jnp.sum(d_second * scaled.astype(F32), 0, keepdims=True),
                jnp.sum(d_second, 0, keepdims=True),
                jnp.sum(d_pre.astype(F32), 0, keepdims=True),
                jnp.zeros((5, D), F32),
            ],
            0,
        )
        up, down, out = dot_tn(second, d_pre), dot_tn(outer, hidden.astype(BF)), dot_tn(outer, mixed_ref[rows, :])
        if slot == 0:
            acc_ref[:, :D] = up
            acc_ref[:, D : 2 * D] = down
            acc_ref[:, 2 * D :] = out
            sums_ref[...] = sums
        else:
            if slot < 3:
                acc_ref[:, :D] += up
                acc_ref[:, D : 2 * D] += down
                acc_ref[:, 2 * D :] += out
            sums_ref[...] += sums
    for total, first, last in ((up, 0, D), (down, D, 2 * D), (out, 2 * D, 1728)):
        total = acc_ref[:, first:last] + total
        for to_x in range(2):
            for plane in range(16):
                row = to_x * 384 + plane * CHUNK
                grad_ref[plane, to_x, :, first:last] = total[row : row + CHUNK].astype(BF)


def backward_rest(outer, second, scaled, mixed, rest, gain, bias):
    outs = [((16, 2, CHUNK, 1728), BF), ((1024, COLS), BF), ((1024, D), BF), ((8, D), F32)]
    return call(
        backward_rest_kernel, outs, (*outer, *second, *scaled, mixed, rest, gain, bias),
        scratch=[pltpu.VMEM((D, 1728), F32)], flops=10**7, limit=B1_LIMIT,
    )


def attend_backward_kernel(
    me_ref, q_ref, k_ref, v_ref, lse_ref, d_mixed_ref, start_ref, cos_ref, sin_ref, turn_ref,
    w_ref, gain_ref, scaled0_ref, scaled1_ref, scaled2_ref, scaled3_ref, part_ref,
    proj_ref, keep_ref, send_ref, sums_ref, bias_ref, dq_ref, dk_ref, dv_ref,
):
    me = me_ref[0]
    for i in reversed(range(4)):
        n = (i + 1) * 256
        rows = slice(i * 256, n)
        there = pl.ds(pl.multiple_of((me ^ i) * 256, 256), 256)
        queries = by_heads(q_ref[rows, :] * BF(0.125))
        upstream = by_heads(d_mixed_ref[there, :])
        k, v = k_ref[:n, :], v_ref[:n, :]
        lse = jnp.concatenate([lse_ref[h : h + 1, rows] for h in range(HEADS_HERE)], 1)
        probability = jnp.exp(dot_nt(k, queries) - lse + blocked(start_ref[:, rows], i, n))
        d_prob = dot_nt(v, upstream)
        row = jnp.sum(probability * d_prob, 0, keepdims=True)
        d_score = (probability * (d_prob - row)).astype(BF)
        dq_ref[rows, :] = own_lanes(dot_tn(d_score, k)) * 0.125
        dk = dot_nn(d_score, queries)
        dv = dot_nn(probability.astype(BF), upstream)
        if i == 3:
            dk_ref[...] = dk
            dv_ref[...] = dv
        else:
            dk_ref[:n, :] += dk
            dv_ref[:n, :] += dv
    turn = turn_ref[...]

    def back(value, cosine, sine):
        upper = value.astype(BF)
        lower = (value - upper.astype(F32)).astype(BF)
        return value * cosine - (dot_nn(upper, turn) + dot_nn(lower, turn)) * sine

    sums = jnp.zeros((8, D), F32)
    bias = jnp.zeros((8, 576), F32)
    for a in range(4):
        there = pl.ds(pl.multiple_of((me ^ a) * 256, 256), 256)
        rows = slice(a * 256, (a + 1) * 256)
        cosine, sine = rope_at(cos_ref, sin_ref, there)
        dq = back(dq_ref[there, :], cosine, sine)
        dk = back(dk_ref[there, :], cosine, sine)
        proj = jnp.concatenate([dq, dk, dv_ref[there, :]], 1).astype(BF)
        proj_ref[rows, :] = proj
        d_first = dot_nt(proj, w_ref[:, 1728:])
        scaled = (scaled0_ref, scaled1_ref, scaled2_ref, scaled3_ref)[a][...]
        weighted = d_first * gain_ref[0:1, :] + part_ref[rows, :].astype(F32)
        if a % 2 == 0:
            keep_ref[a // 2] = weighted
        else:
            send_ref[a // 2] = weighted.astype(BF)
        sums = sums + jnp.concatenate(
            [
                jnp.sum(d_first * scaled.astype(F32), 0, keepdims=True),
                jnp.sum(d_first, 0, keepdims=True),
                jnp.zeros((6, D), F32),
            ],
            0,
        )
        bias = bias + jnp.concatenate(
            [jnp.sum(proj.astype(F32), 0, keepdims=True), jnp.zeros((7, 576), F32)], 0
        )
    sums_ref[...] = sums
    bias_ref[...] = bias


def attend_backward(me, q, k, v, lse, d_mixed, start, cosine, sine, turn, w, gain, scaled, part):
    whole = pl.BlockSpec(memory_space=VMEM)
    ins = (me, q, k, v, lse, d_mixed, start, cosine, sine, turn, w, gain, *scaled, part)
    outs = [((1024, 576), BF), ((2, 256, D), F32), ((2, 256, D), BF), ((8, D), F32), ((8, 576), F32)]
    return call(
        attend_backward_kernel, outs, ins, in_specs=[SMEM_SPEC] + [whole] * 16,
        scratch=[pltpu.VMEM((1024, COLS), F32)] * 3, flops=10**7, limit=B2_LIMIT,
    )


def all_grads_kernel(
    rings, place_ref, first0_ref, first1_ref, first2_ref, first3_ref, proj_ref, sums_ref, sums_rest_ref, bias_ref, upstream_ref, rest_ref, out_ref
):
    first = jnp.concatenate([first0_ref[...], first1_ref[...], first2_ref[...], first3_ref[...]], 0)
    total = dot_tn(first, proj_ref[...])
    pre = sums_rest_ref[2:3, :]
    upper, lower = split(
        jnp.concatenate(
            [
                sums_ref[:2, :],
                sums_rest_ref[:2, :],
                jnp.sum(upstream_ref[...], 0, keepdims=True),
                jnp.concatenate([bias_ref[:1, :], pre[:, :COLS]], 1),
                jnp.concatenate([pre[:, COLS:], jnp.zeros((1, COLS), F32)], 1),
                jnp.zeros((1, D), F32),
            ],
            0,
        )
    )
    row = lax.broadcasted_iota(jnp.int32, (8, 16), 0)
    lane = lax.broadcasted_iota(jnp.int32, (8, 16), 1)
    small = dot_tn(upper, (row == lane).astype(BF)) + dot_tn(lower, (row + 8 == lane).astype(BF))
    x, z, y = place_ref[0], place_ref[1], place_ref[2]
    for to_x in range(2):
        for plane in range(16):
            here = slice(to_x * 384 + plane * CHUNK, to_x * 384 + (plane + 1) * CHUNK)
            place = (plane, to_x)
            if rings:
                half, zr, yr = to_x ^ x, (plane // 4) ^ z, (plane % 4) ^ y
                place = (half, jnp.where(half == 0, yr, zr), jnp.where(half == 0, zr, yr))
            out_ref[(*place, slice(None), slice(0, 1728))] = rest_ref[plane, to_x]
            out_ref[(*place, slice(None), slice(1728, 2304))] = total[here].astype(BF)
            out_ref[(*place, slice(None), slice(2304, 2320))] = small[here].astype(BF)


def all_grads(place, first, proj, parts, rings):
    shape = (2, 4, 4, CHUNK, 2320) if rings else (16, 2, CHUNK, 2320)
    whole = pl.BlockSpec(memory_space=VMEM)
    return call(
        functools.partial(all_grads_kernel, rings), [(shape, BF)], (place, *first, proj, *parts),
        in_specs=[SMEM_SPEC] + [whole] * 10, flops=10**7, limit=GN_LIMIT,
    )[0]


def split(value):
    upper = value.astype(BF)
    return upper, (value - upper.astype(F32)).astype(BF)


def newton_schulz_kernel(
    place_ref, *refs
):
    rows, (small_ref, out_ref, m_ref, g_ref, h_ref, gs_ref, ss_ref, hs_ref, x_ref, xs_ref) = refs[:16], refs[16:]
    x, y = place_ref[0], place_ref[1]
    lane = lax.broadcasted_iota(jnp.int32, (1, D), 1)
    half = y // 2
    used = (x == 0) | ((lane >= half * COLS) & (lane < (half + 1) * COLS))
    for s in range(4):
        for b in range(2):
            for c in range(2):
                m_ref[2 * b + c, s * 192 : (s + 1) * 192, :] = jnp.where(used, rows[8 * b + 2 * s + c][...], jnp.zeros((), BF))

    def store(pair, lower, i, j, value):
        r, c = slice(i * 256, (i + 1) * 256), slice(j * 256, (j + 1) * 256)
        upper_part, lower_part = split(value)
        pair[0, r, c] = upper_part
        pair[1, r, c] = lower_part
        if i != j and lower:
            upper_part, lower_part = split(value.T)
            pair[0, c, r] = upper_part
            pair[1, c, r] = lower_part

    def product(a, b, finish):
        for j in range(3):
            n, c = (j + 1) * 256, slice(j * 256, (j + 1) * 256)
            value = dot_nn(a[0, :n, :], b[0, :, c]) + dot_nn(a[0, :n, :], b[1, :, c]) + dot_nn(a[1, :n, :], b[0, :, c])
            for i in range(j + 1):
                finish(i, j, value[i * 256 : (i + 1) * 256])

    def at(ref, i, j):
        return ref[i * 256 : (i + 1) * 256, j * 256 : (j + 1) * 256]

    def put(ref, i, j, value):
        ref[i * 256 : (i + 1) * 256, j * 256 : (j + 1) * 256] = value

    for j in range(3):
        n, c = (j + 1) * 256, slice(j * 256, (j + 1) * 256)
        value = dot_nt(m_ref[0, :n, :], m_ref[0, c, :])
        for b in range(1, 4):
            value = value + dot_nt(m_ref[b, :n, :], m_ref[b, c, :])
        g_ref[:n, c] = value
    same = lax.broadcasted_iota(jnp.int32, (256, 256), 0) == lax.broadcasted_iota(jnp.int32, (256, 256), 1)

    def trace_of(ref):
        trace = jnp.zeros((1, 1), F32)
        for i in range(3):
            diagonal = jnp.where(same, at(ref, i, i), 0.0)
            trace = trace + jnp.sum(jnp.sum(diagonal, 1, keepdims=True), 0, keepdims=True)
        return trace

    scale = 1.0 / (jnp.sqrt(trace_of(g_ref)) + EPS_ORTH)
    for j in range(3):
        for i in range(j + 1):
            value = at(g_ref, i, j) * (scale * scale)
            put(g_ref, i, j, value)
            store(gs_ref, True, i, j, value)
    which = jnp.where(x == 0, y, half)
    block = jnp.zeros((D, COLS), BF)
    for i in range(4):
        block = jnp.where(which == i, m_ref[0, :, i * COLS : (i + 1) * COLS], block)
    current = block.astype(F32) * scale
    x_ref[...] = current
    xs_ref[0], xs_ref[1] = split(current)

    def mix():
        def finish(i, j, value):
            store(ss_ref, True, i, j, COEF_B * at(g_ref, i, j) + COEF_C * value)

        product(gs_ref, gs_ref, finish)

    def advance():
        s0, s1 = ss_ref[0], ss_ref[1]
        return COEF_A * x_ref[...] + dot_nn(s0, xs_ref[0]) + dot_nn(s0, xs_ref[1]) + dot_nn(s1, xs_ref[0])

    def step():
        mix()
        current = advance()
        x_ref[...] = current
        xs_ref[0], xs_ref[1] = split(current)

        def finish_h(i, j, value):
            value = COEF_A * at(g_ref, i, j) + value
            put(h_ref, i, j, value)
            store(hs_ref, True, i, j, value)

        product(ss_ref, gs_ref, finish_h)

        def finish_g(i, j, value):
            value = COEF_A * at(h_ref, i, j) + value
            put(g_ref, i, j, value)
            store(gs_ref, True, i, j, value)

        product(hs_ref, ss_ref, finish_g)

    def repeated(_, carry):
        step()
        return carry

    lax.fori_loop(0, NS_STEPS - 2, repeated, 0)

    def once(a, b, finish):
        for j in range(3):
            n, c = (j + 1) * 256, slice(j * 256, (j + 1) * 256)
            value = dot_nn(a[0, :n, :], b[0, :, c])
            for i in range(j + 1):
                finish(i, j, value[i * 256 : (i + 1) * 256])

    def store_once(pair, i, j, value):
        r, c = slice(i * 256, (i + 1) * 256), slice(j * 256, (j + 1) * 256)
        pair[0, r, c] = value.astype(BF)
        if i != j:
            pair[0, c, r] = value.T.astype(BF)

    m = trace_of(g_ref) * (1.0 / D)
    for i in range(3):
        value = at(g_ref, i, i) - jnp.where(same, m, 0.0)
        put(g_ref, i, i, value)
        store_once(gs_ref, i, i, value)

    def mix_once(m):
        def finish(i, j, value):
            store(ss_ref, True, i, j, (COEF_B + 2.0 * COEF_C * m) * at(g_ref, i, j) + COEF_C * value)

        once(gs_ref, gs_ref, finish)
        return (COEF_B + COEF_C * m) * m

    def advance_once(p):
        s0, s1 = ss_ref[0], ss_ref[1]
        return (COEF_A + p) * x_ref[...] + dot_nn(s0, xs_ref[0]) + dot_nn(s0, xs_ref[1]) + dot_nn(s1, xs_ref[0])

    p = mix_once(m)
    current = advance_once(p)
    x_ref[...] = current
    xs_ref[0], xs_ref[1] = split(current)

    def mixer_at(i, j):
        r, c = slice(i * 256, (i + 1) * 256), slice(j * 256, (j + 1) * 256)
        return ss_ref[0, r, c].astype(F32) + ss_ref[1, r, c].astype(F32)

    def finish_h_once(i, j, value):
        value = (COEF_A + p) * at(g_ref, i, j) + m * mixer_at(i, j) + value
        put(h_ref, i, j, value)
        store_once(hs_ref, i, j, value)

    once(ss_ref, gs_ref, finish_h_once)
    q = (COEF_A + p) * m

    def finish_g_once(i, j, value):
        value = (COEF_A + p) * at(h_ref, i, j) + q * mixer_at(i, j) + value
        put(g_ref, i, j, value)
        store_once(gs_ref, i, j, value)

    once(hs_ref, ss_ref, finish_g_once)
    p = mix_once((COEF_A + p) * q)
    current = advance_once(p)
    for s in range(4):
        for group in range(8):
            row = s * 192 + group * 24
            out_ref[group, y ^ s, :, :COLS] = current[row : row + 24].astype(BF)
            out_ref[group, y ^ s, :, COLS:] = small_ref[...]


def newton_schulz(place, pieces, small):
    pair = pltpu.VMEM((2, D, D), BF)
    whole = pl.BlockSpec(memory_space=VMEM)
    return call(
        newton_schulz_kernel, [((8, 4, CHUNK, 224), BF)], (place, *pieces, small),
        in_specs=[SMEM_SPEC] + [whole] * 17,
        scratch=[pltpu.VMEM((4, D, D), BF)] + [pltpu.VMEM((D, D), F32)] * 2 + [pair] * 3
        + [pltpu.VMEM((D, COLS), F32), pltpu.VMEM((2, D, COLS), BF)],
        flops=10**7, limit=NS_LIMIT,
    )[0]


def pack_kernel(attn_ref, mlp_ref, out_ref):
    for layer in range(2):
        for m in range(2):
            parts = [mlp_ref[layer, m, :, r, :] for r in range(4)]
            out_ref[layer, :, m * D : (m + 1) * D] = jnp.concatenate(parts, 1).astype(BF)
        parts = [attn_ref[layer, m] for m in (3, 0, 1, 2)]
        out_ref[layer, :, 2 * D :] = jnp.concatenate(parts, 1).astype(BF)


def pack(attn_w, mlp_w):
    return call(pack_kernel, [((2, CHUNK, WIDE), BF)], (attn_w, mlp_w))[0]


def assemble_kernel(place_ref, a0, a1, a2, a2_more, a3, b0, b1, b2, b2_more, b3, out_ref):
    x, z, y = place_ref[0], place_ref[1], place_ref[2]
    for other, blocks in enumerate(((a0, a1, (a2, a2_more), a3), (b0, b1, (b2, b2_more), b3))):
        for outer, block in enumerate(blocks):
            for inner in range(4):
                value = block[inner // 2][inner % 2] if outer == 2 else block[inner]
                zr, yr = (outer, inner) if other else (inner, outer)
                out_ref[(x ^ other) * 16 + (z ^ zr) * 4 + (y ^ yr)] = value


def assemble(place, blocks):
    whole = pl.BlockSpec(memory_space=VMEM)
    return call(
        assemble_kernel, [((32, CHUNK, WIDE), BF)], (place, *blocks), in_specs=[SMEM_SPEC] + [whole] * 10
    )[0]


def momenta_kernel(attn_ref, mlp_ref, grads0_ref, grads1_ref, new_attn_ref, new_mlp_ref, sends_ref, small_ref):
    none = jnp.zeros((CHUNK, 2 * COLS), BF)
    for layer, rest_ref in ((0, grads0_ref), (1, grads1_ref)):
        for m in range(2):
            parts = []
            for r in range(4):
                first = m * D + r * COLS
                mom = MOMENTUM * mlp_ref[layer, m, :, r, :] + rest_ref[:, first : first + COLS]
                new_mlp_ref[layer, m, :, r, :] = mom
                parts.append(mom.astype(BF))
            sends_ref[2 * layer + m] = jnp.concatenate(parts, 1)
        parts = []
        for m in range(4):
            first = 1728 + m * COLS if m < 3 else 2 * D
            grad = rest_ref[:, first : first + COLS]
            mom = MOMENTUM * attn_ref[layer, m] + grad
            new_attn_ref[layer, m] = mom
            parts.append(mom.astype(BF))
        sends_ref[4 + 2 * layer] = jnp.concatenate([*parts[:2], none], 1)
        sends_ref[5 + 2 * layer] = jnp.concatenate([*parts[2:], none], 1)
    here = grads0_ref[:, 2304:2311] + grads0_ref[:, 2312:2319]
    last = grads1_ref[:, 2304:2311] + grads1_ref[:, 2312:2319]
    small_ref[...] = jnp.concatenate([here[:, :5], last[:, :5], here[:, 5:], last[:, 5:]], 1)


def momenta(mom_attn, mom_mlp, *ins):
    outs = [(mom_attn.shape, F32), (mom_mlp.shape, F32), ((8, CHUNK, D), BF), ((CHUNK, 14), F32)]
    return call(momenta_kernel, outs, (mom_attn, mom_mlp, *ins))


def new_weights_kernel(
    back_ref, attn_ref, mlp_ref, mom_bias_ref, bias_ref, mom_vec_ref, vec_ref,
    new_attn_ref, new_mlp_ref, new_mom_bias_ref, new_bias_ref, new_mom_vec_ref, new_vec_ref,
):
    def block(x, z, y):
        return back_ref[x * 16 + z * 4 + y, :, :COLS].astype(F32)

    for layer in range(2):
        for m in range(4):
            step = STEP_SCALE * math.sqrt(D) * block(1, 2 * layer + m // 2, 2 * (m % 2))
            new_attn_ref[layer, m] = attn_ref[layer, m] - step
        for m in range(2):
            for r in range(4):
                step = STEP_SCALE * math.sqrt(FF) * block(0, 2 * layer + m, r)
                new_mlp_ref[layer, m, :, r, :] = mlp_ref[layer, m, :, r, :] - step
    parts = []
    for i in range(32):
        row = lax.broadcasted_iota(jnp.int32, (CHUNK, D), 0)
        lane = lax.broadcasted_iota(jnp.int32, (CHUNK, D), 1)
        parts.append(dot_tn(back_ref[i, :, COLS:], (row + i * CHUNK == lane).astype(BF)))
    lying = sum(parts)
    total = lying[:14] + lying[14:28]
    rate = RATE_VEC / math.sqrt(32768)
    for layer in range(2):
        for row in range(6):
            grad = total[5 * layer + min(row, 4) : 5 * layer + min(row, 4) + 1]
            mom = MOMENTUM * mom_vec_ref[layer, row : row + 1, :] + grad
            new_mom_vec_ref[layer, row : row + 1, :] = mom
            new_vec_ref[layer, row : row + 1, :] = vec_ref[layer, row : row + 1, :] - rate * mom
        grads = jnp.concatenate([total[10 + 2 * layer : 11 + 2 * layer], total[11 + 2 * layer : 12 + 2 * layer]], 1)
        for row in range(7):
            mom = MOMENTUM * mom_bias_ref[layer, row : row + 1, :] + grads[:, row * COLS : (row + 1) * COLS]
            new_mom_bias_ref[layer, row : row + 1, :] = mom
            new_bias_ref[layer, row : row + 1, :] = bias_ref[layer, row : row + 1, :] - rate * mom


def new_weights(*ins):
    return call(new_weights_kernel, [(part.shape, F32) for part in ins[1:]], ins)


def dp_swap(value, mask):
    return lax.ppermute(value, "dp", [(i, i ^ mask) for i in range(32)])


def tensor_swap(value, mask):
    return lax.ppermute(value, "tensor", [(i, i ^ mask) for i in range(4)])


def dp_place():
    me = lax.axis_index("dp")
    return me // 16, (me // 4) % 4, me % 4


def swap_four(pieces, unit):
    return [pieces[0]] + [dp_swap(pieces[s], s * unit) for s in (1, 2, 3)]


PLANE = [[x * 16 + i for i in range(16)] for x in range(2)]


def by_x(own, other):
    x = dp_place()[0]
    return jnp.stack([jnp.where(x == 0, own, other), jnp.where(x == 0, other, own)])


def spread_rows(shard, other):
    return jnp.concatenate([by_x(shard, other)[None]] * 16, 0)


def gather_rows(spread):
    return lax.all_to_all(spread, "dp", 0, 0, tiled=True, axis_index_groups=PLANE)


def gather_by_rings(shard):
    x, z, y = dp_place()
    other = dp_swap(shard, 16)
    halves = []
    for mine, unit, then in ((shard, 4, 1), (other, 1, 4)):
        block = jnp.stack(swap_four([mine] * 4, unit))
        left, right = dp_swap(block, then), dp_swap(block, 3 * then)
        halves += [block, left, dp_swap(right[:2], then), dp_swap(left[2:], 3 * then), right]
    return assemble(jnp.stack([x, z, y]).astype(jnp.int32), halves).reshape(D, WIDE)


def in_order(arrived):
    return arrived.transpose(1, 0, 2, 3).reshape(D, arrived.shape[3])


def scatter_rows(partial):
    return lax.all_to_all(partial, "dp", 0, 0, tiled=True, axis_index_groups=PLANE)


def add_by_rings(partial, ready):
    def total(pieces):
        pieces = [piece.astype(F32) for piece in pieces]
        return (pieces[0] + pieces[1]) + (pieces[2] + pieces[3])

    first = [swap_four([partial[half, s] for s in range(4)], unit) for half, unit in ((0, 1), (1, 4))]
    first, ready = lax.optimization_barrier((first, ready))
    halves = []
    for pieces, then in zip(first, (4, 1)):
        block = total(pieces).astype(BF)
        halves.append(total(swap_four([block[s] for s in range(4)], then)))
    return halves[0] + dp_swap(halves[1].astype(BF), 16).astype(F32), ready


def add_arrived(arrived):
    sums = jnp.sum(arrived.astype(F32), 0)
    x = dp_place()[0]
    other = jnp.where(x == 0, sums[1], sums[0]).astype(BF)
    return jnp.where(x == 0, sums[0], sums[1]) + dp_swap(other, 16).astype(F32)


def gather_tokens(mine, beside=None):
    far = tensor_swap(mine, 2)
    near = tensor_swap(mine, 1)
    if beside is not None:
        far, beside = lax.optimization_barrier((far, beside))
    return [mine, near, far, tensor_swap(far, 1)], beside


def standardize(stream):
    center = stream - jnp.mean(stream, -1, keepdims=True)
    inverse = lax.rsqrt(jnp.mean(center * center, -1, keepdims=True) + EPS_NORM)
    return center * inverse, inverse


def rope_tables(labels):
    kinds = jnp.arange(8, dtype=jnp.int32)
    below = jnp.sum((labels[None, :] < kinds[:, None]).astype(jnp.int32), 1)
    start = jnp.sum(jnp.where(labels[None, :] == kinds[:, None], below[:, None], 0), 0)
    places = jnp.arange(labels.shape[0], dtype=jnp.int32) - start
    frequency = 10000.0 ** (jnp.arange(ROT // 2, dtype=F32) * (-2.0 / ROT))
    angles = places.astype(F32)[None, :] * frequency[:, None]
    cosine, sine = jnp.cos(angles), jnp.sin(angles)
    return jnp.cos(angles), jnp.sin(angles), start[None, :]


def turn_matrix():
    turn = np.zeros((COLS, COLS), np.float32)
    for head in range(HEADS_HERE):
        for i in range(ROT // 2):
            turn[head * HD + i + ROT // 2, head * HD + i] = -1.0
            turn[head * HD + i, head * HD + i + ROT // 2] = 1.0
    return turn


def normalized(stream, vector_rows, beside=None):
    scaled, inverse = standardize(stream)
    first, second, scaled_all = [], [], []
    sent = scaled.astype(jnp.float16)
    if beside is not None:
        sent, beside = lax.optimization_barrier((sent, beside))
        beside = in_order(beside)
    slots, beside = gather_tokens(sent, beside)
    for slot in slots:
        wide = slot.astype(F32)
        first.append((wide * vector_rows[0] + vector_rows[1]).astype(BF))
        second.append((wide * vector_rows[2] + vector_rows[3]).astype(BF))
        scaled_all.append(wide.astype(BF))
    return (scaled, inverse, first, second, scaled_all), beside


def forward_layer(stream, norms, weights, bias_rows, vector_rows, common):
    me, cosine, sine, start, turn = common
    scaled, inverse, first, second, scaled_all = norms
    q, k, v, lse, mixed = attend_forward(
        me, first, weights, bias_rows, turn, cosine, sine, start
    )
    keep_far, send_far = forward_out(second, mixed, weights, bias_rows, 1)
    pair = (keep_far + tensor_swap(send_far, 1).astype(F32)).astype(BF)
    mixed, pair = lax.optimization_barrier((mixed, pair))
    keep, send = forward_out(second, mixed, weights, bias_rows, 0)
    parts = (keep, tensor_swap(send, 1), tensor_swap(pair, 2))
    record = (q, k, v, lse, mixed)
    return record, parts


def add_parts(stream, parts, vector_rows):
    branch = parts[0] + parts[1].astype(F32) + parts[2].astype(F32)
    return stream + branch + vector_rows[4] + vector_rows[5]


def backward_layer(upstream, outer, record, weights, bias_rows, vector_rows, common, ready, last):
    me, cosine, sine, start, turn = common
    scaled, inverse, first, second, scaled_all, q, k, v, lse, mixed = record
    grad_rest, d_mixed, part, sums_rest = backward_rest(
        outer, second, scaled_all, mixed, weights, vector_rows, bias_rows
    )
    if not last:
        d_mixed, ready = lax.optimization_barrier((d_mixed, ready))
    proj, keep, send, sums, bias = attend_backward(
        me, q, k, v, lse, d_mixed, start, cosine, sine, turn, weights, vector_rows, scaled_all, part
    )
    pair = keep + tensor_swap(send, 1).astype(F32)
    pair = (pair[0], pair[1].astype(BF))
    weighted = pair[0] + tensor_swap(pair[1], 2).astype(F32)
    new_upstream = upstream + inverse * (
        weighted
        - jnp.mean(weighted, -1, keepdims=True)
        - scaled * jnp.mean(weighted * scaled, -1, keepdims=True)
    )
    place = jnp.stack(dp_place()).astype(jnp.int32)
    if not last:
        proj, pair = lax.optimization_barrier((proj, pair))
    grads = all_grads(place, first, proj, (sums, sums_rest, bias, upstream, grad_rest), last)
    if last:
        grads, ready = add_by_rings(grads, ready)
    else:
        grads = scatter_rows(grads)
    return new_upstream, grads, ready


def two_terms(value):
    upper = value.astype(BF)
    return jnp.concatenate([upper, (value - upper.astype(F32)).astype(BF)], 1)


def orthogonal_blocks(sends, small):
    x, z, y = dp_place()
    groups = [[i + y_place for i in range(0, 32, 4)] for y_place in range(4)]
    rows = lax.all_to_all(sends, "dp", 0, 0, tiled=True, axis_index_groups=groups).reshape(192, D)
    shared = small[:, :10]
    shared = shared + tensor_swap(shared, 1)
    shared = shared + tensor_swap(shared, 2)
    both = jnp.stack([rows, tensor_swap(rows, 2)])
    left, right = dp_swap(both, 1), dp_swap(both, 3)
    left, shared = lax.optimization_barrier((left, shared))
    pieces = [both[0], both[1], left[0], left[1], dp_swap(right[0], 1), dp_swap(left[1], 3), right[0], right[1]]
    pieces = pieces + [tensor_swap(piece, 1) for piece in pieces]
    small = two_terms(jnp.concatenate([shared, small[:, 10:]], 1))
    small = jnp.pad(small, ((0, 0), (0, 4)))
    result = newton_schulz(jnp.stack([x, y]).astype(jnp.int32), pieces, small)
    return lax.all_to_all(result.reshape(32, CHUNK, 224), "dp", 0, 0, tiled=True)


def per_device(
    x_in, segments, attn_w, mlp_w, in_bias, vectors, mom_attn, mom_mlp, mom_bias, mom_vec, cotangent
):
    cosine, sine, start = rope_tables(segments[0])
    me = lax.axis_index("tensor").astype(jnp.int32).reshape(1)
    common = (me, cosine, sine, start, jnp.asarray(turn_matrix(), BF))
    shards = pack(attn_w, mlp_w)
    arrived = gather_by_rings(shards[0])
    later = spread_rows(shards[1], dp_swap(shards[1], 16))
    stream = x_in[0].astype(F32)
    upstream = cotangent[0]
    norms, _ = normalized(stream, vectors[0])
    arrived, later, norms, common = lax.optimization_barrier((arrived, later, norms, common))
    weights = [arrived]
    arrived = gather_rows(later)
    record, parts = forward_layer(stream, norms, weights[0], in_bias[0], vectors[0], common)
    stream = add_parts(stream, parts, vectors[0])
    saved = [norms + record]
    norms, last = normalized(stream, vectors[1], arrived)
    weights.append(last)
    record, parts = forward_layer(stream, norms, weights[1], in_bias[1], vectors[1], common)
    saved.append(norms + record)
    outer, _ = gather_tokens(upstream.astype(BF))
    upstream, grads_last, ready = backward_layer(
        upstream, outer, saved[1], weights[1], in_bias[1], vectors[1], common, parts, False
    )
    stream = add_parts(stream, ready, vectors[1])
    outer, _ = gather_tokens(upstream.astype(BF))
    upstream, grads_first, grads_last = backward_layer(
        upstream, outer, saved[0], weights[0], in_bias[0], vectors[0], common, grads_last, True
    )
    new_mom_attn, new_mom_mlp, sends, small = momenta(mom_attn, mom_mlp, grads_first, add_arrived(grads_last))
    result = orthogonal_blocks(sends, small)
    new_attn_w, new_mlp_w, new_mom_bias, new_in_bias, new_mom_vec, new_vectors = new_weights(
        result, attn_w, mlp_w, mom_bias, in_bias, mom_vec, vectors
    )
    return (
        stream[None],
        upstream[None],
        new_mom_attn,
        new_attn_w,
        new_mom_mlp,
        new_mlp_w,
        new_mom_bias,
        new_in_bias,
        new_mom_vec,
        new_vectors,
    )


def solution(mesh):
    placed = (
        P("dp", "tensor", None),
        P("dp", None),
        P(None, None, "dp", "tensor"),
        P(None, None, "dp", None, "tensor"),
        P(None, None, "tensor"),
        P(),
        P(None, None, "dp", "tensor"),
        P(None, None, "dp", None, "tensor"),
        P(None, None, "tensor"),
        P(),
        P("dp", "tensor", None),
    )
    return jax.shard_map(
        per_device,
        mesh=mesh,
        in_specs=placed,
        out_specs=(
            P("dp", "tensor", None),
            P("dp", "tensor", None),
            P(None, None, "dp", "tensor"),
            P(None, None, "dp", "tensor"),
            P(None, None, "dp", None, "tensor"),
            P(None, None, "dp", None, "tensor"),
            P(None, None, "tensor"),
            P(None, None, "tensor"),
            P(),
            P(),
        ),
        check_vma=False,
    )
```
